32 devices in a mesh: dp: 8 (over z, y), rep: 4 (over x, core).
Axes of the slice: x: 2, y: 2, z: 4, core: 2. Of those that a mesh axis runs over, the one named last changes fastest.
Arguments:
- queries: bfloat16 [2048, 768], P(('dp', 'rep')), may hold values from -60 to 60
- bank: bfloat16 [64, 4096, 768], P('dp', 'rep'), may hold values from -0.21875 to 0.21875
- labels: int32 [64, 4096], P('dp', 'rep'), may hold values from 0 to 127
- probes: int32 [2048, 8], P(('dp', 'rep')), may hold values from 0 to 63, all different within a row; in each aligned block of 64 rows (0 to 63, 64 to 127, ...) at most 16 rows name the same one
Outputs:
- votes: float32 [2048, 128], P(('dp', 'rep'))
The draws below stay inside these ranges and needn't reach their ends.
Inputs may be any that keep to these rules, and one draw needn't show every extreme that they name: `probes`: each row names 8 different clusters; among the rows of one device no cluster is named more than 16 times.
All inputs are finite; a program needn't handle non-finite values.
Results may differ from the reference program's by a relative error of at most 0.0017.
Values may be sent and summed in bfloat16 or wider, within the bound.
A program may use at most 192 MiB of HBM per device.

```python
import math
import jax
import jax.numpy as jnp
import numpy as np
from jax import lax

D = 768
CLASSES = 128
P_SIZE = 8
R = 4096
Q_DEV = 64
CLUSTERS = 64
QUERIES = 2048
CAP = 16
N_DP = 8
N_REP = 4


def draw_queries(key, part):
    first_key = jax.random.fold_in(jax.random.fold_in(key, 11), 0)
    values = jnp.clip(jax.random.normal(first_key, (QUERIES, D), jnp.float32), -6.0, 6.0)
    return values.astype(jnp.bfloat16)


def touch_ends(values, key, least, top_value):
    longest = values.shape.index(max(values.shape))
    spots = []
    for shift in (0, 1):
        where = [jax.random.randint(jax.random.fold_in(key, axis), (), 0, length) for axis, length in enumerate(values.shape)]
        where[longest] = (where[longest] + shift) % values.shape[longest]
        spots.append(tuple(where))
    return values.at[spots[0]].set(least).at[spots[1]].set(top_value)


def shard_levels(key, shape, shards, low, high):
    def one(axis_at, blocks):
        steps = jax.random.uniform(jax.random.fold_in(jax.random.fold_in(key, 6), axis_at), (blocks,), jnp.float32, low / len(shards), high / len(shards))
        return jnp.repeat(jnp.exp(steps), shape[axis_at] // blocks).reshape((-1,) + (1,) * (len(shape) - axis_at - 1))

    factor_of = one(*shards[0])
    for cut in shards[1:]:
        factor_of = factor_of * one(*cut)
    return factor_of


def routed_block(stream_key, own, number, rows, number_of, top, reach, slope):
    ranking = jax.random.permutation(stream_key, number_of)
    heavy_load, common = portions_of(number_of, rows * top, reach, slope, True), portions_of(number_of, rows * top, reach, slope, False)
    places = jnp.arange(number_of)

    def named(sizes, turn):
        used = int((sizes > 0).sum())
        fixed = max(1, used // 4)
        passed = fixed + (places - fixed + turn * (used - fixed)) % max(1, number_of - fixed)
        return jnp.zeros((number_of,), jnp.int32).at[ranking[jnp.where(places < fixed, places, passed)]].set(jnp.asarray(sizes, jnp.int32))

    sizes = jnp.where(number % 4 == 0, named(heavy_load, number // 4), named(common, number - number // 4 - 1))
    mixed = jax.random.permutation(jax.random.fold_in(own, 3), number_of)
    source_of, taker = mixed[0:number_of // 2 * 2:2], mixed[1:number_of // 2 * 2:2]
    slack = jnp.minimum(sizes[source_of] - 1, reach - sizes[taker]) // 2
    slack = jnp.where((source_of == ranking[0]) | (taker == ranking[0]) | (sizes[taker] == 0), 0, jnp.maximum(slack, 0))
    passed = jax.random.randint(jax.random.fold_in(own, 4), (number_of // 2,), 0, 1 << 20) % (slack + 1)
    sizes = sizes.at[source_of].add(-passed).at[taker].add(passed)
    members = jnp.searchsorted(jnp.cumsum(sizes), jnp.arange(rows * top), side="right").astype(jnp.int32)
    grid = members.reshape(top, rows).T
    grid = grid[jax.random.permutation(jax.random.fold_in(own, 1), rows)]
    turn = jax.random.randint(jax.random.fold_in(own, 2), (rows, 1), 0, top)
    return jnp.take_along_axis(grid, (jnp.arange(top)[None, :] + turn) % top, axis=1)


def portions_of(number_of, total, most, lean, full):
    weights = [(1 << 20) // math.isqrt(rank ** lean) + 1 for rank in range(1, number_of + 1)]
    largest = most if full else min(most, max(-(-total // number_of), total * weights[0] // sum(weights)))
    least = 1 if total - largest >= number_of - 1 else 0
    counts, rest = [largest] + [least] * (number_of - 1), total - largest - least * (number_of - 1)
    while rest > 0:
        candidates = [i for i in range(1, number_of) if counts[i] < largest] or [i for i in range(1, number_of) if counts[i] < most]
        whole, left = sum([weights[i] for i in candidates]), rest
        for i in candidates:
            addition = min(most - counts[i], max(1, left * weights[i] // whole), rest)
            counts[i] = counts[i] + addition
            rest = rest - addition
    return np.array(counts)


def centred(stream_key, shape, scale, reach, cuts=(), kind=jnp.bfloat16):
    array = scale * jax.random.normal(stream_key, shape, jnp.float32)
    if cuts:
        array = array * shard_levels(stream_key, shape, cuts, -0.22, 0.18)
    return jnp.clip(array, -reach, reach).astype(kind)


def setup_inputs(seed: int = 0) -> dict:
    splits = jax.random.split(jax.random.key(seed), 5)
    queries = draw_queries(jax.random.fold_in(splits[4], 71), 0)
    bank = centred(splits[1], (CLUSTERS, R, D), D ** -0.5, 0.21875, ((0, 8), (1, 4)))
    labels = touch_ends(jax.random.randint(splits[2], (CLUSTERS, R), 0, CLASSES), jax.random.fold_in(splits[2], 1), 0, CLASSES - 1).astype(jnp.int32)
    probes_keys = jax.random.split(jax.random.fold_in(splits[3], 1), QUERIES // Q_DEV)
    probes_turns = jax.random.permutation(jax.random.fold_in(splits[3], 3), QUERIES // Q_DEV)
    probes = jax.vmap(lambda own, number: routed_block(jax.random.fold_in(splits[3], 2), own, number, Q_DEV, CLUSTERS, P_SIZE, CAP, 2))(probes_keys, probes_turns).reshape((QUERIES, P_SIZE))
    return dict(queries=queries, bank=bank, labels=labels, probes=probes)


logit_scale = 2.0


def reference(queries, bank, labels, probes):
    limit = CAP * N_DP * N_REP
    class_iota = jnp.arange(CLASSES, dtype=jnp.int32)

    def visit(carry, cluster):
        top_now, total_now, tally_now = carry
        member = jnp.any(probes == cluster, axis=1)
        order = jnp.argsort(jnp.where(member, 0, 1).astype(jnp.int32), stable=True)[:limit].astype(jnp.int32)
        valid = member[order]
        picked = queries[order]
        cluster_rows = lax.dynamic_index_in_dim(bank, cluster, 0, keepdims=False)
        row_labels = lax.dynamic_index_in_dim(labels, cluster, 0, keepdims=False)
        scores = logit_scale * jnp.dot(picked, cluster_rows.T, preferred_element_type=jnp.float32)
        highest = jnp.max(scores, axis=1)
        weights = jnp.exp(scores - highest[:, None])
        totals = jnp.sum(weights, axis=1)
        weights_half = weights.astype(jnp.bfloat16)
        one_hot = (row_labels[:, None] == class_iota[None, :]).astype(jnp.bfloat16)
        tallies = jnp.dot(weights_half, one_hot, preferred_element_type=jnp.float32)
        old_top = top_now[order]
        new_top = jnp.where(valid, jnp.maximum(old_top, highest), old_top)
        keep_weight = jnp.exp(old_top - new_top)
        add_weight = jnp.where(valid, jnp.exp(highest - new_top), jnp.zeros_like(highest))
        new_total = total_now[order] * keep_weight + totals * add_weight
        new_tally = tally_now[order] * keep_weight[:, None] + tallies * add_weight[:, None]
        return (top_now.at[order].set(new_top), total_now.at[order].set(new_total), tally_now.at[order].set(new_tally)), None

    start_state = (jnp.full((QUERIES,), -1.0e30, jnp.float32), jnp.zeros((QUERIES,), jnp.float32), jnp.zeros((QUERIES, CLASSES), jnp.float32))
    final_state, _ = lax.scan(visit, start_state, jnp.arange(CLUSTERS, dtype=jnp.int32))
    return CLASSES * final_state[2] / final_state[1][:, None]
```

```python
import functools

import jax
import jax.numpy as jnp
from jax import lax
from jax.experimental import pallas as pl
from jax.experimental.pallas import tpu as pltpu
from jax.sharding import PartitionSpec as P

CLASSES = 128
LANES = 128
LOGIT_SCALE = 2.0
LOW = -3.0e38
MESH = pl.DeviceIdType.MESH


def kernel(cfg, msg_ref, labels_ref, bank_ref, out_ref,
           bank_v, code, qs, s_buf, top_b, tot_b, tal, send_t, send_s,
           recv_t, recv_s, pair_out, pair_in, turned,
           bank_sem, st_sem, ss_sem, rt_sem, rs_sem, ps_sem, pr_sem):
    n_rep, n, q, cap, clusters, rows, depth, probe_count, group = cfg
    groups, width, span = n // group, group * q, group * cap
    pieces = depth // LANES
    me_dp, me_rep = lax.axis_index("dp"), lax.axis_index("rep")
    me = me_dp * n_rep + me_rep
    my_group, my_place = me // group, lax.rem(me, group)

    def device(flat):
        return (flat // n_rep, lax.rem(flat, n_rep))

    for c in range(clusters):
        pltpu.make_async_copy(bank_ref.at[c], bank_v.at[c], bank_sem.at[c]).start()

    barrier = pltpu.get_barrier_semaphore()

    def greet(flat):
        pl.semaphore_signal(barrier, inc=1, device_id=device(flat), device_id_type=MESH)

    for j in range(1, groups):
        greet(lax.rem(my_group + j, groups) * group + my_place)
    for j in range(1, group):
        greet(my_group * group + lax.rem(my_place + j, group))
    pl.semaphore_wait(barrier, groups + group - 2)

    lane = lax.broadcasted_iota(jnp.int32, (width, width), 1)
    row = lax.broadcasted_iota(jnp.int32, (width, width), 0)
    before = jnp.where((row < lane) & (row // q == lane // q), 1.0, 0.0).astype(jnp.bfloat16)
    offset = (lax.broadcasted_iota(jnp.int32, (1, width), 1) // q) * cap
    slot_iota = lax.broadcasted_iota(jnp.int32, (span, width), 0)
    first = me_dp * clusters

    def pick(g, _):
        named = msg_ref[g * group, pieces * q : pieces * q + 16, :].astype(jnp.float32)
        for j in range(1, group):
            named = jnp.maximum(
                named, msg_ref[g * group + j, pieces * q : pieces * q + 16, :].astype(jnp.float32))
        if width != LANES:
            named = jnp.concatenate(
                [msg_ref[g * group + j, pieces * q : pieces * q + 16, :].astype(jnp.float32)[:, :q]
                 for j in range(group)], axis=1)
        members = [
            jnp.max(jnp.where(named == (first + c).astype(jnp.float32), 1.0, 0.0), axis=0, keepdims=True)
            for c in range(clusters)
        ]
        member = jnp.concatenate(members, axis=0)
        rank = jnp.dot(member.astype(jnp.bfloat16), before, preferred_element_type=jnp.float32)
        place = jnp.where(member > 0.5, rank.astype(jnp.int32) + offset, -1)
        code[g] = place
        hot = jnp.concatenate(
            [jnp.where(slot_iota == place[c : c + 1, :], LOGIT_SCALE, 0.0) for c in range(clusters)], axis=0
        ).astype(jnp.bfloat16)
        block = jnp.concatenate(
            [
                jnp.concatenate(
                    [msg_ref[g * group + j, p * q : (p + 1) * q, :] for p in range(pieces)], axis=1)
                for j in range(group)
            ],
            axis=0,
        )
        picked = jnp.dot(hot, block, preferred_element_type=jnp.float32).astype(jnp.bfloat16)
        for c in range(clusters):
            qs[c, g] = picked[c * span : (c + 1) * span]
        return 0

    lax.fori_loop(0, groups, pick, 0)

    half = groups // 2
    slots = half * span
    class_iota = lax.broadcasted_iota(jnp.int32, (CLASSES, rows), 0)

    def score(c, h):
        picked = qs[c, h * half : (h + 1) * half].reshape(slots, depth)
        s_buf[h] = lax.dot_general(
            picked, bank_v[c], (((1,), (1,)), ((), ())), preferred_element_type=jnp.float32)

    def weigh(c, h):
        s = s_buf[h]
        top = jnp.max(s, axis=1, keepdims=True)
        e = jnp.exp(s - top)
        total = jnp.sum(e, axis=1, keepdims=True)
        hot = jnp.where(class_iota == labels_ref[pl.ds(c, 1), :], 1.0, 0.0).astype(jnp.bfloat16)
        tally = lax.dot_general(
            e.astype(jnp.bfloat16), hot, (((1,), (1,)), ((), ())), preferred_element_type=jnp.float32)
        where = slice(h * half, (h + 1) * half)
        top_b[c, where] = jnp.broadcast_to(top, (slots, LANES)).reshape(half, span, LANES)
        tot_b[c, where] = jnp.broadcast_to(total, (slots, LANES)).reshape(half, span, LANES)
        tal[c, where] = tally.reshape(half, span, CLASSES)

    def wait_bank(c):
        pltpu.make_async_copy(bank_ref.at[c], bank_v.at[c], bank_sem.at[c]).wait()

    wait_bank(0)
    score(0, 0)

    def cluster(c, _):
        score(c, 1)
        weigh(c, 0)

        @pl.when(c + 1 < clusters)
        def _():
            wait_bank(c + 1)

        score(jnp.minimum(c + 1, clusters - 1), 0)
        weigh(c, 1)
        return 0

    lax.fori_loop(0, clusters, cluster, 0)

    def copies(g):
        target = device(g * group + my_place)
        return (
            pltpu.make_async_remote_copy(
                src_ref=send_t.at[g], dst_ref=recv_t.at[my_group], send_sem=st_sem.at[g],
                recv_sem=rt_sem.at[my_group], device_id=target, device_id_type=MESH),
            pltpu.make_async_remote_copy(
                src_ref=send_s.at[g], dst_ref=recv_s.at[my_group], send_sem=ss_sem.at[g],
                recv_sem=rs_sem.at[my_group], device_id=target, device_id_type=MESH),
        )

    wide = max(1, width // LANES)

    def merge(j, _):
        g = lax.rem(my_group + j, groups)
        place = code[g]
        hots, tops = [], []
        for c in range(clusters):
            hot = slot_iota == place[c : c + 1, :]
            hots.append(hot)
            here = jnp.concatenate([top_b[c, g]] * wide, axis=1)
            tops.append(jnp.max(jnp.where(hot, here, LOW), axis=0, keepdims=True))
        highest = functools.reduce(jnp.maximum, tops)
        total = jnp.zeros((1, width), jnp.float32)
        scaled = []
        for c in range(clusters):
            w = jnp.exp(tops[c] - highest)
            here = jnp.concatenate([tot_b[c, g]] * wide, axis=1)
            total = total + w * jnp.sum(jnp.where(hots[c], here, 0.0), axis=0, keepdims=True)
            scaled.append(jnp.where(hots[c], w, 0.0))
        weight = jnp.concatenate(scaled, axis=0)
        tally = jnp.concatenate([tal[c, g] for c in range(clusters)], axis=0)
        w_hi = weight.astype(jnp.bfloat16)
        w_lo = (weight - w_hi.astype(jnp.float32)).astype(jnp.bfloat16)
        t_hi = tally.astype(jnp.bfloat16)
        t_lo = (tally - t_hi.astype(jnp.float32)).astype(jnp.bfloat16)

        def turn(a, b):
            return lax.dot_general(a, b, (((0,), (0,)), ((), ())), preferred_element_type=jnp.float32)

        merged = turn(t_hi, w_hi) + (turn(t_hi, w_lo) + turn(t_lo, w_hi))
        stats = jnp.concatenate([highest, total] + [jnp.zeros((1, width), jnp.float32)] * 6, axis=0)

        send_t[g] = merged.astype(jnp.bfloat16)
        send_s[g] = stats

        @pl.when(j < groups)
        def _():
            for copy in copies(g):
                copy.start()

        return 0

    lax.fori_loop(1, groups + 1, merge, 0)
    recv_t[my_group] = send_t[my_group]
    recv_s[my_group] = send_s[my_group]

    def arrived(j, _):
        g = lax.rem(my_group + groups - j, groups)
        pltpu.make_async_remote_copy(
            src_ref=send_t.at[g], dst_ref=recv_t.at[g], send_sem=st_sem.at[g],
            recv_sem=rt_sem.at[g], device_id=device(g * group + my_place), device_id_type=MESH).wait_recv()
        pltpu.make_async_remote_copy(
            src_ref=send_s.at[g], dst_ref=recv_s.at[g], send_sem=ss_sem.at[g],
            recv_sem=rs_sem.at[g], device_id=device(g * group + my_place), device_id_type=MESH).wait_recv()
        return 0

    lax.fori_loop(1, groups, arrived, 0)

    highest = functools.reduce(jnp.maximum, [recv_s[g, 0:1, :] for g in range(groups)])
    total = jnp.zeros((1, width), jnp.float32)
    merged = jnp.zeros((CLASSES, width), jnp.float32)
    for g in range(groups):
        w = jnp.exp(recv_s[g, 0:1, :] - highest)
        total = total + w * recv_s[g, 1:2, :]
        merged = merged + w * recv_t[g].astype(jnp.float32)
    pair_out[0:CLASSES, :] = merged
    pair_out[CLASSES : CLASSES + 8, :] = jnp.concatenate(
        [highest, total] + [jnp.zeros((1, width), jnp.float32)] * 6, axis=0)

    def pair(j):
        return pltpu.make_async_remote_copy(
            src_ref=pair_out, dst_ref=pair_in.at[j], send_sem=ps_sem.at[j], recv_sem=pr_sem.at[j],
            device_id=device(my_group * group + lax.rem(my_place + j, group)), device_id_type=MESH)

    for j in range(1, group):
        pair(j).start()
    for j in range(1, group):
        pair(j).wait_recv()
    tops = [highest] + [pair_in[j, CLASSES : CLASSES + 1, :] for j in range(1, group)]
    best = functools.reduce(jnp.maximum, tops)
    w = jnp.exp(highest - best)
    total, merged = total * w, merged * w
    for j in range(1, group):
        w = jnp.exp(tops[j] - best)
        total = total + w * pair_in[j, CLASSES + 1 : CLASSES + 2, :]
        merged = merged + w * pair_in[j, 0:CLASSES, :]
    turned[...] = (CLASSES * merged / total).T
    out_ref[...] = turned[pl.ds(pl.multiple_of(my_place * q, q), q), :]

    def sent(j, _):
        for copy in copies(lax.rem(my_group + j, groups)):
            copy.wait_send()
        return 0

    lax.fori_loop(1, groups, sent, 0)
    for j in range(1, group):
        pair(j).wait_send()


def local(queries, bank, labels, probes):
    q, depth = queries.shape
    probe_count = probes.shape[1]
    clusters, rows, _ = bank.shape
    n_dp, n_rep = lax.axis_size("dp"), lax.axis_size("rep")
    n = n_dp * n_rep
    cap = 2 * q * probe_count // (clusters * n_dp)
    group = max(LANES // q, 16 // cap)
    groups, width, span = n // group, group * q, group * cap
    pieces = depth // LANES

    place = lax.rem(lax.axis_index("rep"), group)
    named = jnp.full((16, LANES), -1, jnp.bfloat16)
    shift = place * q if width == LANES else 0
    named = lax.dynamic_update_slice(named, probes.T.astype(jnp.bfloat16), (0, shift))
    message = jnp.concatenate(
        [queries[:, p * LANES : (p + 1) * LANES] for p in range(pieces)] + [named], axis=0)
    messages = lax.all_gather(message, ("dp", "rep"), axis=0)

    cfg = (n_rep, n, q, cap, clusters, rows, depth, probe_count, group)
    vmem = pl.BlockSpec(memory_space=pltpu.VMEM)
    f32, bf16 = jnp.float32, jnp.bfloat16
    return pl.pallas_call(
        functools.partial(kernel, cfg),
        out_shape=jax.ShapeDtypeStruct((q, CLASSES), f32),
        in_specs=[vmem, vmem, pl.BlockSpec(memory_space=pl.ANY)],
        out_specs=vmem,
        scratch_shapes=[
            pltpu.VMEM((clusters, rows, depth), bf16),
            pltpu.VMEM((groups, clusters, width), jnp.int32),
            pltpu.VMEM((clusters, groups, span, depth), bf16),
            pltpu.VMEM((2, groups // 2 * span, rows), f32),
            pltpu.VMEM((clusters, groups, span, LANES), f32),
            pltpu.VMEM((clusters, groups, span, LANES), f32),
            pltpu.VMEM((clusters, groups, span, CLASSES), f32),
            pltpu.VMEM((groups, CLASSES, width), bf16),
            pltpu.VMEM((groups, 8, width), f32),
            pltpu.VMEM((groups, CLASSES, width), bf16),
            pltpu.VMEM((groups, 8, width), f32),
            pltpu.VMEM((CLASSES + 8, width), f32),
            pltpu.VMEM((group, CLASSES + 8, width), f32),
            pltpu.VMEM((width, CLASSES), f32),
            pltpu.SemaphoreType.DMA((clusters,)),
            pltpu.SemaphoreType.DMA((groups,)),
            pltpu.SemaphoreType.DMA((groups,)),
            pltpu.SemaphoreType.DMA((groups,)),
            pltpu.SemaphoreType.DMA((groups,)),
            pltpu.SemaphoreType.DMA((group,)),
            pltpu.SemaphoreType.DMA((group,)),
        ],
        compiler_params=pltpu.CompilerParams(
            collective_id=0, has_side_effects=True, vmem_limit_bytes=56 * 1024 * 1024),
    )(messages, labels, bank)


def solution(mesh):
    return jax.shard_map(
        local,
        mesh=mesh,
        in_specs=(
            P(("dp", "rep"), None),
            P("dp", "rep", None),
            P("dp", "rep"),
            P(("dp", "rep"), None),
        ),
        out_specs=P(("dp", "rep"), None),
        check_vma=False,
    )
```

```python
import functools

import jax
import jax.numpy as jnp
from jax import lax
from jax.experimental import pallas as pl
from jax.experimental.pallas import tpu as pltpu
from jax.sharding import PartitionSpec as P

CLASSES = 128
LANES = 128
LOGIT_SCALE = 2.0
LOW = -3.0e38
MESH = pl.DeviceIdType.MESH


def kernel(cfg, query_ref, probe_ref, labels_ref, bank_ref, out_ref,
           msg_ref, bank_v, code, qs, s_buf, top_b, tot_b, tal, send_t, send_s,
           recv_t, recv_s, pair_out, pair_in, turned,
           bank_sem, go_sem, come_sem, st_sem, ss_sem, rt_sem, rs_sem, ps_sem, pr_sem):
    n_rep, n, q, cap, clusters, rows, depth, probe_count, group = cfg
    groups, width, span = n // group, group * q, group * cap
    pieces = depth // LANES
    me_dp, me_rep = lax.axis_index("dp"), lax.axis_index("rep")
    me = me_dp * n_rep + me_rep
    my_group, my_place = me // group, lax.rem(me, group)

    def device(flat):
        return (flat // n_rep, lax.rem(flat, n_rep))

    for c in range(clusters):
        pltpu.make_async_copy(bank_ref.at[c], bank_v.at[c], bank_sem.at[c]).start()

    barrier = pltpu.get_barrier_semaphore()

    def greet(flat):
        pl.semaphore_signal(barrier, inc=1, device_id=device(flat), device_id_type=MESH)

    for j in range(1, groups):
        greet(lax.rem(my_group + j, groups) * group + my_place)
    for j in range(1, group):
        greet(my_group * group + lax.rem(my_place + j, group))
    pl.semaphore_wait(barrier, groups + group - 2)

    line, z, y = lax.axis_size("dp") // 2, me_dp // 2, lax.rem(me_dp, 2)
    x, core = me_rep // 2, lax.rem(me_rep, 2)
    height = pieces * q + 16
    cut = height // 32 * 16
    whole, upper, lower = (0, height), (0, cut), (cut, height - cut)

    def at(z_, y_, x_, core_):
        return (z_ * 2 + y_) * n_rep + x_ * 2 + core_

    def move(block, part, kind, target):
        return pltpu.make_async_remote_copy(
            src_ref=msg_ref.at[block, pl.ds(*part)], dst_ref=msg_ref.at[block, pl.ds(*part)],
            send_sem=go_sem.at[block, kind], recv_sem=come_sem.at[block, 1 if part == lower else 0],
            device_id=device(target), device_id_type=MESH)

    sibling, over_x, over_y = at(z, y, x, 1 - core), at(z, y, 1 - x, core), at(z, 1 - y, x, core)
    started = []

    def start(condition, block, part, kind, target):
        def run():
            move(block, part, kind, target).start()

        pl.when(condition)(run)
        started.append((condition, block, part, kind, target))

    def wait_for(condition, block, part, source):
        def run():
            move(block, part, 0, source).wait_recv()

        pl.when(condition)(run)

    def fan_out(b, there):
        block = at(b, y, x, core)
        start(there, block, whole, 2, over_x)
        start(there, block, whole, 3, over_y)
        start(there, block, whole, 4, sibling)

    def step_line(t):
        for b, there, source, onward, kind in (
            (z - t, z - t >= 0, z - 1, z + 1, 0),
            (z + t, z + t < line, z + 1, z - 1, 1),
        ):
            block = at(b, y, x, core)
            wait_for(there, block, whole, at(source, y, x, core))
            start(there & (onward >= 0) & (onward < line), block, whole, kind, at(onward, y, x, core))
            fan_out(b, there)

    def both(t):
        if t == 0:
            return ((z, z >= 0),)
        return ((z - t, z - t >= 0), (z + t, z + t < line))

    def step_cross(t):
        for b, there in both(t):
            block = at(b, y, 1 - x, core)
            wait_for(there, block, whole, over_x)
            start(there, block, upper, 3, over_y)
            start(there, block, whole, 4, sibling)
            block = at(b, 1 - y, x, core)
            wait_for(there, block, whole, over_y)
            start(there, block, lower, 2, over_x)
            start(there, block, whole, 4, sibling)

    def step_corner(t):
        for b, there in both(t):
            block = at(b, 1 - y, 1 - x, core)
            wait_for(there, block, upper, over_y)
            start(there, block, upper, 3, sibling)
            wait_for(there, block, lower, over_x)
            start(there, block, lower, 4, sibling)

    def step_sibling(t):
        for b, there in both(t):
            wait_for(there, at(b, y, x, 1 - core), whole, sibling)
            wait_for(there, at(b, y, 1 - x, 1 - core), whole, sibling)
            wait_for(there, at(b, 1 - y, x, 1 - core), whole, sibling)
            wait_for(there, at(b, 1 - y, 1 - x, 1 - core), upper, sibling)
            wait_for(there, at(b, 1 - y, 1 - x, 1 - core), lower, sibling)

    for p in range(pieces):
        msg_ref[me, p * q : (p + 1) * q, :] = query_ref[:, p * LANES : (p + 1) * LANES]
    shift = my_place * q if width == LANES else 0
    spread = lax.broadcasted_iota(jnp.int32, (q, LANES), 1) == (
        lax.broadcasted_iota(jnp.int32, (q, LANES), 0) + shift)
    raised = jnp.concatenate(
        [(probe_ref[...] + 1).astype(jnp.float32), jnp.zeros((q, 16 - probe_count), jnp.float32)],
        axis=1).astype(jnp.bfloat16)
    named_here = lax.dot_general(
        raised, jnp.where(spread, 1.0, 0.0).astype(jnp.bfloat16), (((0,), (0,)), ((), ())),
        preferred_element_type=jnp.float32)
    msg_ref[me, pieces * q : height, :] = (named_here - 1.0).astype(jnp.bfloat16)

    start(z + 1 < line, me, whole, 0, at(z + 1, y, x, core))
    start(z >= 1, me, whole, 1, at(z - 1, y, x, core))
    fan_out(z, z >= 0)
    for t in range(line + 2):
        if 1 <= t < line:
            step_line(t)
        if 1 <= t <= line:
            step_cross(t - 1)
        if t >= 2:
            step_corner(t - 2)
    for t in range(line):
        step_sibling(t)

    lane = lax.broadcasted_iota(jnp.int32, (width, width), 1)
    row = lax.broadcasted_iota(jnp.int32, (width, width), 0)
    before = jnp.where((row < lane) & (row // q == lane // q), 1.0, 0.0).astype(jnp.bfloat16)
    offset = (lax.broadcasted_iota(jnp.int32, (1, width), 1) // q) * cap
    slot_iota = lax.broadcasted_iota(jnp.int32, (span, width), 0)
    first = me_dp * clusters

    def pick(g, _):
        named = msg_ref[g * group, pieces * q : pieces * q + 16, :].astype(jnp.float32)
        for j in range(1, group):
            named = jnp.maximum(
                named, msg_ref[g * group + j, pieces * q : pieces * q + 16, :].astype(jnp.float32))
        if width != LANES:
            named = jnp.concatenate(
                [msg_ref[g * group + j, pieces * q : pieces * q + 16, :].astype(jnp.float32)[:, :q]
                 for j in range(group)], axis=1)
        members = [
            jnp.max(jnp.where(named == (first + c).astype(jnp.float32), 1.0, 0.0), axis=0, keepdims=True)
            for c in range(clusters)
        ]
        member = jnp.concatenate(members, axis=0)
        rank = jnp.dot(member.astype(jnp.bfloat16), before, preferred_element_type=jnp.float32)
        place = jnp.where(member > 0.5, rank.astype(jnp.int32) + offset, -1)
        code[g] = place
        hot = jnp.concatenate(
            [jnp.where(slot_iota == place[c : c + 1, :], LOGIT_SCALE, 0.0) for c in range(clusters)], axis=0
        ).astype(jnp.bfloat16)
        block = jnp.concatenate(
            [
                jnp.concatenate(
                    [msg_ref[g * group + j, p * q : (p + 1) * q, :] for p in range(pieces)], axis=1)
                for j in range(group)
            ],
            axis=0,
        )
        picked = jnp.dot(hot, block, preferred_element_type=jnp.float32).astype(jnp.bfloat16)
        for c in range(clusters):
            qs[c, g] = picked[c * span : (c + 1) * span]
        return 0

    lax.fori_loop(0, groups, pick, 0)

    half = groups // 2
    slots = half * span
    class_iota = lax.broadcasted_iota(jnp.int32, (CLASSES, rows), 0)

    def score(c, h):
        picked = qs[c, h * half : (h + 1) * half].reshape(slots, depth)
        s_buf[h] = lax.dot_general(
            picked, bank_v[c], (((1,), (1,)), ((), ())), preferred_element_type=jnp.float32)

    def weigh(c, h):
        s = s_buf[h]
        top = jnp.max(s, axis=1, keepdims=True)
        e = jnp.exp(s - top)
        total = jnp.sum(e, axis=1, keepdims=True)
        hot = jnp.where(class_iota == labels_ref[pl.ds(c, 1), :], 1.0, 0.0).astype(jnp.bfloat16)
        tally = lax.dot_general(
            e.astype(jnp.bfloat16), hot, (((1,), (1,)), ((), ())), preferred_element_type=jnp.float32)
        where = slice(h * half, (h + 1) * half)
        top_b[c, where] = jnp.broadcast_to(top, (slots, LANES)).reshape(half, span, LANES)
        tot_b[c, where] = jnp.broadcast_to(total, (slots, LANES)).reshape(half, span, LANES)
        tal[c, where] = tally.reshape(half, span, CLASSES)

    def wait_bank(c):
        pltpu.make_async_copy(bank_ref.at[c], bank_v.at[c], bank_sem.at[c]).wait()

    wait_bank(0)
    score(0, 0)

    def cluster(c, _):
        score(c, 1)
        weigh(c, 0)

        @pl.when(c + 1 < clusters)
        def _():
            wait_bank(c + 1)

        score(jnp.minimum(c + 1, clusters - 1), 0)
        weigh(c, 1)
        return 0

    lax.fori_loop(0, clusters, cluster, 0)

    def copies(g):
        target = device(g * group + my_place)
        return (
            pltpu.make_async_remote_copy(
                src_ref=send_t.at[g], dst_ref=recv_t.at[my_group], send_sem=st_sem.at[g],
                recv_sem=rt_sem.at[my_group], device_id=target, device_id_type=MESH),
            pltpu.make_async_remote_copy(
                src_ref=send_s.at[g], dst_ref=recv_s.at[my_group], send_sem=ss_sem.at[g],
                recv_sem=rs_sem.at[my_group], device_id=target, device_id_type=MESH),
        )

    wide = max(1, width // LANES)

    def merge(j, _):
        g = lax.rem(my_group + j, groups)
        place = code[g]
        hots, tops = [], []
        for c in range(clusters):
            hot = slot_iota == place[c : c + 1, :]
            hots.append(hot)
            here = jnp.concatenate([top_b[c, g]] * wide, axis=1)
            tops.append(jnp.max(jnp.where(hot, here, LOW), axis=0, keepdims=True))
        highest = functools.reduce(jnp.maximum, tops)
        total = jnp.zeros((1, width), jnp.float32)
        scaled = []
        for c in range(clusters):
            w = jnp.exp(tops[c] - highest)
            here = jnp.concatenate([tot_b[c, g]] * wide, axis=1)
            total = total + w * jnp.sum(jnp.where(hots[c], here, 0.0), axis=0, keepdims=True)
            scaled.append(jnp.where(hots[c], w, 0.0))
        weight = jnp.concatenate(scaled, axis=0)
        tally = jnp.concatenate([tal[c, g] for c in range(clusters)], axis=0)
        w_hi = weight.astype(jnp.bfloat16)
        w_lo = (weight - w_hi.astype(jnp.float32)).astype(jnp.bfloat16)
        t_hi = tally.astype(jnp.bfloat16)
        t_lo = (tally - t_hi.astype(jnp.float32)).astype(jnp.bfloat16)

        def turn(a, b):
            return lax.dot_general(a, b, (((0,), (0,)), ((), ())), preferred_element_type=jnp.float32)

        merged = turn(t_hi, w_hi) + (turn(t_hi, w_lo) + turn(t_lo, w_hi))
        stats = jnp.concatenate([highest, total] + [jnp.zeros((1, width), jnp.float32)] * 6, axis=0)

        send_t[g] = merged.astype(jnp.bfloat16)
        send_s[g] = stats

        @pl.when(j < groups)
        def _():
            for copy in copies(g):
                copy.start()

        return 0

    lax.fori_loop(1, groups + 1, merge, 0)
    recv_t[my_group] = send_t[my_group]
    recv_s[my_group] = send_s[my_group]

    def arrived(j, _):
        g = lax.rem(my_group + groups - j, groups)
        pltpu.make_async_remote_copy(
            src_ref=send_t.at[g], dst_ref=recv_t.at[g], send_sem=st_sem.at[g],
            recv_sem=rt_sem.at[g], device_id=device(g * group + my_place), device_id_type=MESH).wait_recv()
        pltpu.make_async_remote_copy(
            src_ref=send_s.at[g], dst_ref=recv_s.at[g], send_sem=ss_sem.at[g],
            recv_sem=rs_sem.at[g], device_id=device(g * group + my_place), device_id_type=MESH).wait_recv()
        return 0

    lax.fori_loop(1, groups, arrived, 0)

    highest = functools.reduce(jnp.maximum, [recv_s[g, 0:1, :] for g in range(groups)])
    total = jnp.zeros((1, width), jnp.float32)
    merged = jnp.zeros((CLASSES, width), jnp.float32)
    for g in range(groups):
        w = jnp.exp(recv_s[g, 0:1, :] - highest)
        total = total + w * recv_s[g, 1:2, :]
        merged = merged + w * recv_t[g].astype(jnp.float32)
    pair_out[0:CLASSES, :] = merged
    pair_out[CLASSES : CLASSES + 8, :] = jnp.concatenate(
        [highest, total] + [jnp.zeros((1, width), jnp.float32)] * 6, axis=0)

    def pair(j):
        return pltpu.make_async_remote_copy(
            src_ref=pair_out, dst_ref=pair_in.at[j], send_sem=ps_sem.at[j], recv_sem=pr_sem.at[j],
            device_id=device(my_group * group + lax.rem(my_place + j, group)), device_id_type=MESH)

    for j in range(1, group):
        pair(j).start()
    for j in range(1, group):
        pair(j).wait_recv()
    tops = [highest] + [pair_in[j, CLASSES : CLASSES + 1, :] for j in range(1, group)]
    best = functools.reduce(jnp.maximum, tops)
    w = jnp.exp(highest - best)
    total, merged = total * w, merged * w
    for j in range(1, group):
        w = jnp.exp(tops[j] - best)
        total = total + w * pair_in[j, CLASSES + 1 : CLASSES + 2, :]
        merged = merged + w * pair_in[j, 0:CLASSES, :]
    turned[...] = (CLASSES * merged / total).T
    out_ref[...] = turned[pl.ds(pl.multiple_of(my_place * q, q), q), :]

    for condition, block, part, kind, target in started:
        def run(block=block, part=part, kind=kind, target=target):
            move(block, part, kind, target).wait_send()

        pl.when(condition)(run)

    def sent(j, _):
        for copy in copies(lax.rem(my_group + j, groups)):
            copy.wait_send()
        return 0

    lax.fori_loop(1, groups, sent, 0)
    for j in range(1, group):
        pair(j).wait_send()


def local(queries, bank, labels, probes):
    q, depth = queries.shape
    probe_count = probes.shape[1]
    clusters, rows, _ = bank.shape
    n_dp, n_rep = lax.axis_size("dp"), lax.axis_size("rep")
    n = n_dp * n_rep
    cap = 2 * q * probe_count // (clusters * n_dp)
    group = max(LANES // q, 16 // cap)
    groups, width, span = n // group, group * q, group * cap
    pieces = depth // LANES

    cfg = (n_rep, n, q, cap, clusters, rows, depth, probe_count, group)
    vmem = pl.BlockSpec(memory_space=pltpu.VMEM)
    f32, bf16 = jnp.float32, jnp.bfloat16
    return pl.pallas_call(
        functools.partial(kernel, cfg),
        out_shape=jax.ShapeDtypeStruct((q, CLASSES), f32),
        in_specs=[vmem, vmem, vmem, pl.BlockSpec(memory_space=pl.ANY)],
        out_specs=vmem,
        scratch_shapes=[
            pltpu.VMEM((n, pieces * q + 16, LANES), bf16),
            pltpu.VMEM((clusters, rows, depth), bf16),
            pltpu.VMEM((groups, clusters, width), jnp.int32),
            pltpu.VMEM((clusters, groups, span, depth), bf16),
            pltpu.VMEM((2, groups // 2 * span, rows), f32),
            pltpu.VMEM((clusters, groups, span, LANES), f32),
            pltpu.VMEM((clusters, groups, span, LANES), f32),
            pltpu.VMEM((clusters, groups, span, CLASSES), f32),
            pltpu.VMEM((groups, CLASSES, width), bf16),
            pltpu.VMEM((groups, 8, width), f32),
            pltpu.VMEM((groups, CLASSES, width), bf16),
            pltpu.VMEM((groups, 8, width), f32),
            pltpu.VMEM((CLASSES + 8, width), f32),
            pltpu.VMEM((group, CLASSES + 8, width), f32),
            pltpu.VMEM((width, CLASSES), f32),
            pltpu.SemaphoreType.DMA((clusters,)),
            pltpu.SemaphoreType.DMA((n, 5)),
            pltpu.SemaphoreType.DMA((n, 2)),
            pltpu.SemaphoreType.DMA((groups,)),
            pltpu.SemaphoreType.DMA((groups,)),
            pltpu.SemaphoreType.DMA((groups,)),
            pltpu.SemaphoreType.DMA((groups,)),
            pltpu.SemaphoreType.DMA((group,)),
            pltpu.SemaphoreType.DMA((group,)),
        ],
        compiler_params=pltpu.CompilerParams(
            collective_id=0, has_side_effects=True, vmem_limit_bytes=56 * 1024 * 1024),
    )(queries, probes, labels, bank)


def solution(mesh):
    return jax.shard_map(
        local,
        mesh=mesh,
        in_specs=(
            P(("dp", "rep"), None),
            P("dp", "rep", None),
            P("dp", "rep"),
            P(("dp", "rep"), None),
        ),
        out_specs=P(("dp", "rep"), None),
        check_vma=False,
    )
```

```python
import functools

import jax
import jax.numpy as jnp
from jax import lax
from jax.experimental import pallas as pl
from jax.experimental.pallas import tpu as pltpu
from jax.sharding import PartitionSpec as P

CLASSES = 128
LANES = 128
LOGIT_SCALE = 2.0
LOW = -3.0e38
MESH = pl.DeviceIdType.MESH


def kernel(cfg, query_ref, probe_ref, labels_ref, bank_ref, out_ref,
           msg_ref, bank_v, code, qs, s_buf, top_b, tot_b, tal, send_t, send_s,
           recv_t, recv_s, pair_out, pair_in, turned,
           bank_sem, go_sem, come_sem, st_sem, ss_sem, rt_sem, rs_sem, ps_sem, pr_sem):
    n_rep, n, q, cap, clusters, rows, depth, probe_count, group = cfg
    groups, width, span = n // group, group * q, group * cap
    pieces = depth // LANES
    me_dp, me_rep = lax.axis_index("dp"), lax.axis_index("rep")
    me = me_dp * n_rep + me_rep
    my_group, my_place = me // group, lax.rem(me, group)

    def device(flat):
        return (flat // n_rep, lax.rem(flat, n_rep))

    for c in range(clusters):
        pltpu.make_async_copy(bank_ref.at[c], bank_v.at[c], bank_sem.at[c]).start()

    barrier = pltpu.get_barrier_semaphore()

    def greet(flat):
        pl.semaphore_signal(barrier, inc=1, device_id=device(flat), device_id_type=MESH)

    for j in range(1, groups):
        greet(lax.rem(my_group + j, groups) * group + my_place)
    for j in range(1, group):
        greet(my_group * group + lax.rem(my_place + j, group))
    pl.semaphore_wait(barrier, groups + group - 2)

    line, z, y = lax.axis_size("dp") // 2, me_dp // 2, lax.rem(me_dp, 2)
    x, core = me_rep // 2, lax.rem(me_rep, 2)
    height = pieces * q + 16
    cut = height // 32 * 16
    whole, upper, lower = (0, height), (0, cut), (cut, height - cut)

    def at(z_, y_, x_, core_):
        return (z_ * 2 + y_) * n_rep + x_ * 2 + core_

    def move(block, part, kind, target):
        return pltpu.make_async_remote_copy(
            src_ref=msg_ref.at[block, pl.ds(*part)], dst_ref=msg_ref.at[block, pl.ds(*part)],
            send_sem=go_sem.at[block, kind], recv_sem=come_sem.at[block, 1 if part == lower else 0],
            device_id=device(target), device_id_type=MESH)

    sibling, over_x, over_y = at(z, y, x, 1 - core), at(z, y, 1 - x, core), at(z, 1 - y, x, core)
    ending = []

    def start(condition, block, part, kind, target):
        def run():
            copy = move(block, part, kind, target)
            if ending:
                copy.wait_send()
            else:
                copy.start()

        pl.when(condition)(run)

    def wait_for(condition, block, part, source):
        def run():
            move(block, part, 0, source).wait_recv()

        if not ending:
            pl.when(condition)(run)

    def fan_out(b, there):
        block = at(b, y, x, core)
        start(there, block, whole, 2, over_x)
        start(there, block, whole, 3, over_y)
        start(there, block, whole, 4, sibling)

    def step_line(t):
        for b, there, source, onward, kind in (
            (z - t, z - t >= 0, z - 1, z + 1, 0),
            (z + t, z + t < line, z + 1, z - 1, 1),
        ):
            block = at(b, y, x, core)
            wait_for(there, block, whole, at(source, y, x, core))
            start(there & (onward >= 0) & (onward < line), block, whole, kind, at(onward, y, x, core))
            fan_out(b, there)

    def both(t, near):
        if t == 0:
            return ((z, z >= 0),) if near else ()
        spots = ((z - t, z - t >= 0), (z + t, z + t < line))
        mine = z // (line // 2)
        if near:
            return tuple((b, there & (b // (line // 2) == mine)) for b, there in spots)
        return tuple((b, there & (b // (line // 2) != mine)) for b, there in spots)

    def step_cross(t, near):
        for b, there in both(t, near):
            block = at(b, y, 1 - x, core)
            wait_for(there, block, whole, over_x)
            start(there, block, upper, 3, over_y)
            start(there, block, whole, 4, sibling)
            block = at(b, 1 - y, x, core)
            wait_for(there, block, whole, over_y)
            start(there, block, lower, 2, over_x)
            start(there, block, whole, 4, sibling)

    def step_corner(t, near):
        for b, there in both(t, near):
            block = at(b, 1 - y, 1 - x, core)
            wait_for(there, block, upper, over_y)
            start(there, block, upper, 3, sibling)
            wait_for(there, block, lower, over_x)
            start(there, block, lower, 4, sibling)

    def step_sibling(t, near):
        for b, there in both(t, near):
            wait_for(there, at(b, y, x, 1 - core), whole, sibling)
            wait_for(there, at(b, y, 1 - x, 1 - core), whole, sibling)
            wait_for(there, at(b, 1 - y, x, 1 - core), whole, sibling)
            wait_for(there, at(b, 1 - y, 1 - x, 1 - core), upper, sibling)
            wait_for(there, at(b, 1 - y, 1 - x, 1 - core), lower, sibling)

    for p in range(pieces):
        msg_ref[me, p * q : (p + 1) * q, :] = query_ref[:, p * LANES : (p + 1) * LANES]
    shift = my_place * q if width == LANES else 0
    spread = lax.broadcasted_iota(jnp.int32, (q, LANES), 1) == (
        lax.broadcasted_iota(jnp.int32, (q, LANES), 0) + shift)
    raised = jnp.concatenate(
        [(probe_ref[...] + 1).astype(jnp.float32), jnp.zeros((16 - probe_count, q), jnp.float32)],
        axis=0).astype(jnp.bfloat16)
    named_here = jnp.dot(
        raised, jnp.where(spread, 1.0, 0.0).astype(jnp.bfloat16), preferred_element_type=jnp.float32)
    msg_ref[me, pieces * q : height, :] = (named_here - 1.0).astype(jnp.bfloat16)

    def step_own():
        start(z + 1 < line, me, whole, 0, at(z + 1, y, x, core))
        start(z >= 1, me, whole, 1, at(z - 1, y, x, core))
        fan_out(z, z >= 0)

    step_own()
    close = line // 2
    for t in range(line):
        if t >= 1:
            step_line(t)
        if t < close:
            step_cross(t, True)
        if 1 <= t <= close:
            step_corner(t - 1, True)
    for t in range(close):
        step_sibling(t, True)

    def serve_cross():
        for t in range(1, line):
            step_cross(t, False)

    def serve_corner():
        for t in range(1, line):
            step_corner(t, False)

    lane = lax.broadcasted_iota(jnp.int32, (width, width), 1)
    row = lax.broadcasted_iota(jnp.int32, (width, width), 0)
    before = jnp.where((row < lane) & (row // q == lane // q), 1.0, 0.0).astype(jnp.bfloat16)
    offset = (lax.broadcasted_iota(jnp.int32, (1, width), 1) // q) * cap
    slot_iota = lax.broadcasted_iota(jnp.int32, (span, width), 0)
    first = me_dp * clusters

    def pick(i, base):
        g = base + i
        named = msg_ref[g * group, pieces * q : pieces * q + 16, :].astype(jnp.float32)
        for j in range(1, group):
            named = jnp.maximum(
                named, msg_ref[g * group + j, pieces * q : pieces * q + 16, :].astype(jnp.float32))
        if width != LANES:
            named = jnp.concatenate(
                [msg_ref[g * group + j, pieces * q : pieces * q + 16, :].astype(jnp.float32)[:, :q]
                 for j in range(group)], axis=1)
        members = [
            jnp.max(jnp.where(named == (first + c).astype(jnp.float32), 1.0, 0.0), axis=0, keepdims=True)
            for c in range(clusters)
        ]
        member = jnp.concatenate(members, axis=0)
        rank = jnp.dot(member.astype(jnp.bfloat16), before, preferred_element_type=jnp.float32)
        place = jnp.where(member > 0.5, rank.astype(jnp.int32) + offset, -1)
        code[g] = place
        hot = jnp.concatenate(
            [jnp.where(slot_iota == place[c : c + 1, :], LOGIT_SCALE, 0.0) for c in range(clusters)], axis=0
        ).astype(jnp.bfloat16)
        block = jnp.concatenate(
            [
                jnp.concatenate(
                    [msg_ref[g * group + j, p * q : (p + 1) * q, :] for p in range(pieces)], axis=1)
                for j in range(group)
            ],
            axis=0,
        )
        picked = jnp.dot(hot, block, preferred_element_type=jnp.float32).astype(jnp.bfloat16)
        for c in range(clusters):
            qs[c, g] = picked[c * span : (c + 1) * span]
        return base

    half = groups // 2
    slots = half * span
    class_iota = lax.broadcasted_iota(jnp.int32, (CLASSES, rows), 0)

    def score(c, base, buffer):
        picked = qs[c, pl.ds(base, half)].reshape(slots, depth)
        s_buf[buffer] = lax.dot_general(
            picked, bank_v[c], (((1,), (1,)), ((), ())), preferred_element_type=jnp.float32)

    def weigh(c, base, buffer):
        s = s_buf[buffer]
        top = jnp.max(s, axis=1, keepdims=True)
        e = jnp.exp(s - top)
        total = jnp.sum(e, axis=1, keepdims=True)
        hot = jnp.where(class_iota == labels_ref[pl.ds(c, 1), :], 1.0, 0.0).astype(jnp.bfloat16)
        tally = lax.dot_general(
            e.astype(jnp.bfloat16), hot, (((1,), (1,)), ((), ())), preferred_element_type=jnp.float32)
        where = pl.ds(base, half)
        top_b[c, where] = jnp.broadcast_to(top, (slots, LANES)).reshape(half, span, LANES)
        tot_b[c, where] = jnp.broadcast_to(total, (slots, LANES)).reshape(half, span, LANES)
        tal[c, where] = tally.reshape(half, span, CLASSES)

    def wait_bank(c):
        pltpu.make_async_copy(bank_ref.at[c], bank_v.at[c], bank_sem.at[c]).wait()

    def phase(base, near):
        if near:
            wait_bank(0)
        score(0, base, 0)

        def cluster(i, _):
            c = 2 * i
            if near:
                wait_bank(c + 1)
                wait_bank(c + 2)
                pl.when(c == clusters // 4)(serve_cross)
                pl.when(c == clusters // 2)(serve_corner)
            score(c + 1, base, 1)
            weigh(c, base, 0)
            score(c + 2, base, 0)
            weigh(c + 1, base, 1)
            return 0

        lax.fori_loop(0, clusters // 2 - 1, cluster, 0)
        if near:
            wait_bank(clusters - 1)
        score(clusters - 1, base, 1)
        weigh(clusters - 2, base, 0)
        weigh(clusters - 1, base, 1)

    def copies(g):
        target = device(g * group + my_place)
        return (
            pltpu.make_async_remote_copy(
                src_ref=send_t.at[g], dst_ref=recv_t.at[my_group], send_sem=st_sem.at[g],
                recv_sem=rt_sem.at[my_group], device_id=target, device_id_type=MESH),
            pltpu.make_async_remote_copy(
                src_ref=send_s.at[g], dst_ref=recv_s.at[my_group], send_sem=ss_sem.at[g],
                recv_sem=rs_sem.at[my_group], device_id=target, device_id_type=MESH),
        )

    wide = max(1, width // LANES)

    def merge(j, base):
        g = base + lax.rem(my_group + j, half)
        place = code[g]
        hots, tops = [], []
        for c in range(clusters):
            hot = slot_iota == place[c : c + 1, :]
            hots.append(hot)
            here = jnp.concatenate([top_b[c, g]] * wide, axis=1)
            tops.append(jnp.max(jnp.where(hot, here, LOW), axis=0, keepdims=True))
        highest = functools.reduce(jnp.maximum, tops)
        total = jnp.zeros((1, width), jnp.float32)
        scaled = []
        for c in range(clusters):
            w = jnp.exp(tops[c] - highest)
            here = jnp.concatenate([tot_b[c, g]] * wide, axis=1)
            total = total + w * jnp.sum(jnp.where(hots[c], here, 0.0), axis=0, keepdims=True)
            scaled.append(jnp.where(hots[c], w, 0.0))
        weight = jnp.concatenate(scaled, axis=0)
        tally = jnp.concatenate([tal[c, g] for c in range(clusters)], axis=0)
        w_hi = weight.astype(jnp.bfloat16)
        w_lo = (weight - w_hi.astype(jnp.float32)).astype(jnp.bfloat16)
        t_hi = tally.astype(jnp.bfloat16)
        t_lo = (tally - t_hi.astype(jnp.float32)).astype(jnp.bfloat16)

        def turn(a, b):
            return lax.dot_general(a, b, (((0,), (0,)), ((), ())), preferred_element_type=jnp.float32)

        merged = turn(t_hi, w_hi) + (turn(t_hi, w_lo) + turn(t_lo, w_hi))
        stats = jnp.concatenate([highest, total] + [jnp.zeros((1, width), jnp.float32)] * 6, axis=0)

        send_t[g] = merged.astype(jnp.bfloat16)
        send_s[g] = stats

        @pl.when(g != my_group)
        def _():
            for copy in copies(g):
                copy.start()

        return base

    near_base = my_group // half * half
    far_base = half - near_base
    lax.fori_loop(0, half, pick, near_base)
    phase(near_base, True)
    lax.fori_loop(1, half + 1, merge, near_base)
    for t in range(1, line):
        step_sibling(t, False)
    lax.fori_loop(0, half, pick, far_base)
    phase(far_base, False)
    lax.fori_loop(1, half + 1, merge, far_base)

    def gathered(state, place):
        highest, total, merged = state
        stats, tally = place
        best = jnp.maximum(highest, stats[0:1, :])
        keep, w = jnp.exp(highest - best), jnp.exp(stats[0:1, :] - best)
        return (best, total * keep + w * stats[1:2, :], merged * keep + w * tally.astype(jnp.float32))

    def arrived(base):
        def one(j, state):
            g = base + lax.rem(my_group + 2 * half - j, half)
            for copy in (
                pltpu.make_async_remote_copy(
                    src_ref=send_t.at[g], dst_ref=recv_t.at[g], send_sem=st_sem.at[g], recv_sem=rt_sem.at[g],
                    device_id=device(g * group + my_place), device_id_type=MESH),
                pltpu.make_async_remote_copy(
                    src_ref=send_s.at[g], dst_ref=recv_s.at[g], send_sem=ss_sem.at[g], recv_sem=rs_sem.at[g],
                    device_id=device(g * group + my_place), device_id_type=MESH),
            ):
                copy.wait_recv()
            return gathered(state, (recv_s[g], recv_t[g]))

        return one

    own = send_s[my_group]
    state = (own[0:1, :], own[1:2, :], send_t[my_group].astype(jnp.float32))
    state = lax.fori_loop(1, half, arrived(near_base), state)
    state = lax.fori_loop(1, half + 1, arrived(far_base), state)
    highest, total, merged = state
    pair_out[0:CLASSES, :] = merged
    pair_out[CLASSES : CLASSES + 8, :] = jnp.concatenate(
        [highest, total] + [jnp.zeros((1, width), jnp.float32)] * 6, axis=0)

    def pair(j):
        return pltpu.make_async_remote_copy(
            src_ref=pair_out, dst_ref=pair_in.at[j], send_sem=ps_sem.at[j], recv_sem=pr_sem.at[j],
            device_id=device(my_group * group + lax.rem(my_place + j, group)), device_id_type=MESH)

    for j in range(1, group):
        pair(j).start()
    for j in range(1, group):
        pair(j).wait_recv()
    tops = [highest] + [pair_in[j, CLASSES : CLASSES + 1, :] for j in range(1, group)]
    best = functools.reduce(jnp.maximum, tops)
    w = jnp.exp(highest - best)
    total, merged = total * w, merged * w
    for j in range(1, group):
        w = jnp.exp(tops[j] - best)
        total = total + w * pair_in[j, CLASSES + 1 : CLASSES + 2, :]
        merged = merged + w * pair_in[j, 0:CLASSES, :]
    turned[...] = (merged / total).T
    out_ref[...] = turned[pl.ds(pl.multiple_of(my_place * q, q), q), :]

    ending.append(True)
    step_own()
    for t in range(line):
        if t >= 1:
            step_line(t)
        for near in (True, False):
            step_cross(t, near)
            step_corner(t, near)

    def sent(j, _):
        for copy in copies(lax.rem(my_group + j, groups)):
            copy.wait_send()
        return 0

    lax.fori_loop(1, groups, sent, 0)
    for j in range(1, group):
        pair(j).wait_send()


def local(queries, bank, labels, probes):
    q, depth = queries.shape
    probe_count = probes.shape[1]
    clusters, rows, _ = bank.shape
    n_dp, n_rep = lax.axis_size("dp"), lax.axis_size("rep")
    n = n_dp * n_rep
    cap = 2 * q * probe_count // (clusters * n_dp)
    group = max(LANES // q, 16 // cap)
    groups, width, span = n // group, group * q, group * cap
    pieces = depth // LANES

    cfg = (n_rep, n, q, cap, clusters, rows, depth, probe_count, group)
    vmem = pl.BlockSpec(memory_space=pltpu.VMEM)
    f32, bf16 = jnp.float32, jnp.bfloat16
    return pl.pallas_call(
        functools.partial(kernel, cfg),
        out_shape=jax.ShapeDtypeStruct((q, CLASSES), f32),
        in_specs=[vmem, vmem, vmem, pl.BlockSpec(memory_space=pl.ANY)],
        out_specs=vmem,
        scratch_shapes=[
            pltpu.VMEM((n, pieces * q + 16, LANES), bf16),
            pltpu.VMEM((clusters, rows, depth), bf16),
            pltpu.VMEM((groups, clusters, width), jnp.int32),
            pltpu.VMEM((clusters, groups, span, depth), bf16),
            pltpu.VMEM((2, groups // 2 * span, rows), f32),
            pltpu.VMEM((clusters, groups, span, LANES), f32),
            pltpu.VMEM((clusters, groups, span, LANES), f32),
            pltpu.VMEM((clusters, groups, span, CLASSES), f32),
            pltpu.VMEM((groups, CLASSES, width), bf16),
            pltpu.VMEM((groups, 8, width), f32),
            pltpu.VMEM((groups, CLASSES, width), bf16),
            pltpu.VMEM((groups, 8, width), f32),
            pltpu.VMEM((CLASSES + 8, width), f32),
            pltpu.VMEM((group, CLASSES + 8, width), f32),
            pltpu.VMEM((width, CLASSES), f32),
            pltpu.SemaphoreType.DMA((clusters,)),
            pltpu.SemaphoreType.DMA((n, 5)),
            pltpu.SemaphoreType.DMA((n, 2)),
            pltpu.SemaphoreType.DMA((groups,)),
            pltpu.SemaphoreType.DMA((groups,)),
            pltpu.SemaphoreType.DMA((groups,)),
            pltpu.SemaphoreType.DMA((groups,)),
            pltpu.SemaphoreType.DMA((group,)),
            pltpu.SemaphoreType.DMA((group,)),
        ],
        compiler_params=pltpu.CompilerParams(
            collective_id=0, has_side_effects=True, vmem_limit_bytes=56 * 1024 * 1024),
    )(queries, probes.T, labels, bank) * CLASSES


def solution(mesh):
    return jax.shard_map(
        local,
        mesh=mesh,
        in_specs=(
            P(("dp", "rep"), None),
            P("dp", "rep", None),
            P("dp", "rep"),
            P(("dp", "rep"), None),
        ),
        out_specs=P(("dp", "rep"), None),
        check_vma=False,
    )
```

```python
import functools

import jax
import jax.numpy as jnp
from jax import lax
from jax.experimental import pallas as pl
from jax.experimental.pallas import tpu as pltpu
from jax.sharding import PartitionSpec as P

CLASSES = 128
LANES = 128
LOGIT_SCALE = 2.0
LOW = -3.0e38
MESH = pl.DeviceIdType.MESH


def kernel(cfg, query_ref, probe_ref, labels_ref, bank_ref, out_ref,
           msg_ref, bank_v, code, qs, s_buf, top_b, tot_b, tal, send_t, send_s,
           recv_t, recv_s, pair_out, pair_in, turned,
           bank_sem, go_sem, come_sem, st_sem, ss_sem, rt_sem, rs_sem, ps_sem, pr_sem):
    n_rep, n, q, cap, clusters, rows, depth, probe_count, group = cfg
    groups, width, span = n // group, group * q, group * cap
    pieces = depth // LANES
    me_dp, me_rep = lax.axis_index("dp"), lax.axis_index("rep")
    me = me_dp * n_rep + me_rep
    my_group, my_place = me // group, lax.rem(me, group)

    def device(flat):
        return (flat // n_rep, lax.rem(flat, n_rep))

    for c in range(clusters):
        pltpu.make_async_copy(bank_ref.at[c], bank_v.at[c], bank_sem.at[c]).start()

    barrier = pltpu.get_barrier_semaphore()

    def greet(flat):
        pl.semaphore_signal(barrier, inc=1, device_id=device(flat), device_id_type=MESH)

    for j in range(1, groups):
        greet(lax.rem(my_group + j, groups) * group + my_place)
    for j in range(1, group):
        greet(my_group * group + lax.rem(my_place + j, group))
    pl.semaphore_wait(barrier, groups + group - 2)

    line, z, y = lax.axis_size("dp") // 2, me_dp // 2, lax.rem(me_dp, 2)
    x, core = me_rep // 2, lax.rem(me_rep, 2)
    height = pieces * q + 16
    cut = height // 32 * 16
    whole, upper, lower = (0, height), (0, cut), (cut, height - cut)

    def at(z_, y_, x_, core_):
        return (z_ * 2 + y_) * n_rep + x_ * 2 + core_

    def move(block, part, kind, target):
        return pltpu.make_async_remote_copy(
            src_ref=msg_ref.at[block, pl.ds(*part)], dst_ref=msg_ref.at[block, pl.ds(*part)],
            send_sem=go_sem.at[block, kind], recv_sem=come_sem.at[block, 1 if part == lower else 0],
            device_id=device(target), device_id_type=MESH)

    sibling, over_x, over_y = at(z, y, x, 1 - core), at(z, y, 1 - x, core), at(z, 1 - y, x, core)
    ending = []

    def start(condition, block, part, kind, target):
        def run():
            copy = move(block, part, kind, target)
            if ending:
                copy.wait_send()
            else:
                copy.start()

        pl.when(condition)(run)

    def wait_for(condition, block, part, source):
        def run():
            move(block, part, 0, source).wait_recv()

        if not ending:
            pl.when(condition)(run)

    def fan_out(b, there):
        block = at(b, y, x, core)
        start(there, block, whole, 2, over_x)
        start(there, block, whole, 3, over_y)
        start(there, block, whole, 4, sibling)

    def step_line(t):
        for b, there, source, onward, kind in (
            (z - t, z - t >= 0, z - 1, z + 1, 0),
            (z + t, z + t < line, z + 1, z - 1, 1),
        ):
            block = at(b, y, x, core)
            wait_for(there, block, whole, at(source, y, x, core))
            start(there & (onward >= 0) & (onward < line), block, whole, kind, at(onward, y, x, core))
            fan_out(b, there)

    def both(t, near):
        if t == 0:
            return ((z, z >= 0),) if near else ()
        spots = ((z - t, z - t >= 0), (z + t, z + t < line))
        mine = z // (line // 2)
        if near:
            return tuple((b, there & (b // (line // 2) == mine)) for b, there in spots)
        return tuple((b, there & (b // (line // 2) != mine)) for b, there in spots)

    def step_cross(t, near):
        for b, there in both(t, near):
            block = at(b, y, 1 - x, core)
            wait_for(there, block, whole, over_x)
            start(there, block, upper, 3, over_y)
            start(there, block, whole, 4, sibling)
            block = at(b, 1 - y, x, core)
            wait_for(there, block, whole, over_y)
            start(there, block, lower, 2, over_x)
            start(there, block, whole, 4, sibling)

    def step_corner(t, near):
        for b, there in both(t, near):
            block = at(b, 1 - y, 1 - x, core)
            wait_for(there, block, upper, over_y)
            start(there, block, upper, 3, sibling)
            wait_for(there, block, lower, over_x)
            start(there, block, lower, 4, sibling)

    def step_sibling(t, near):
        for b, there in both(t, near):
            wait_for(there, at(b, y, x, 1 - core), whole, sibling)
            wait_for(there, at(b, y, 1 - x, 1 - core), whole, sibling)
            wait_for(there, at(b, 1 - y, x, 1 - core), whole, sibling)
            wait_for(there, at(b, 1 - y, 1 - x, 1 - core), upper, sibling)
            wait_for(there, at(b, 1 - y, 1 - x, 1 - core), lower, sibling)

    for p in range(pieces):
        msg_ref[me, p * q : (p + 1) * q, :] = query_ref[:, p * LANES : (p + 1) * LANES]
    shift = my_place * q if width == LANES else 0
    spread = lax.broadcasted_iota(jnp.int32, (q, LANES), 1) == (
        lax.broadcasted_iota(jnp.int32, (q, LANES), 0) + shift)
    raised = jnp.concatenate(
        [(probe_ref[...] + 1).astype(jnp.float32), jnp.zeros((16 - probe_count, q), jnp.float32)],
        axis=0).astype(jnp.bfloat16)
    named_here = jnp.dot(
        raised, jnp.where(spread, 1.0, 0.0).astype(jnp.bfloat16), preferred_element_type=jnp.float32)
    msg_ref[me, pieces * q : height, :] = (named_here - 1.0).astype(jnp.bfloat16)

    def step_own():
        start(z + 1 < line, me, whole, 0, at(z + 1, y, x, core))
        start(z >= 1, me, whole, 1, at(z - 1, y, x, core))
        fan_out(z, z >= 0)

    step_own()
    close = line // 2
    for t in range(line):
        if t >= 1:
            step_line(t)
        if t < close:
            step_cross(t, True)
        if 1 <= t <= close:
            step_corner(t - 1, True)
    for t in range(close):
        step_sibling(t, True)

    def serve_cross():
        for t in range(1, line):
            step_cross(t, False)

    def serve_corner():
        for t in range(1, line):
            step_corner(t, False)

    lane = lax.broadcasted_iota(jnp.int32, (width, width), 1)
    row = lax.broadcasted_iota(jnp.int32, (width, width), 0)
    before = jnp.where((row < lane) & (row // q == lane // q), 1.0, 0.0).astype(jnp.bfloat16)
    offset = (lax.broadcasted_iota(jnp.int32, (1, width), 1) // q) * cap
    slot_iota = lax.broadcasted_iota(jnp.int32, (span, width), 0)
    first = me_dp * clusters
    probe_rows = 16
    half = groups // 2
    batch = 4 if half % 4 == 0 else 1

    def members_of(g):
        blocks = [msg_ref[g * group + j, pieces * q : pieces * q + probe_rows, :].astype(jnp.float32)
                  for j in range(group)]
        if width == LANES:
            named = functools.reduce(jnp.maximum, blocks)
        else:
            named = jnp.concatenate([block[:, :q] for block in blocks], axis=1)
        return [
            jnp.max(jnp.where(named == (first + c).astype(jnp.float32), 1.0, 0.0), axis=0, keepdims=True)
            for c in range(clusters)
        ]

    def pick(i, base):
        gs = [base + i * batch + k for k in range(batch)]
        member = jnp.concatenate([m for g in gs for m in members_of(g)], axis=0)
        rank = jnp.dot(member.astype(jnp.bfloat16), before, preferred_element_type=jnp.float32)
        places = jnp.where(member > 0.5, rank.astype(jnp.int32) + offset, -1)
        picks = []
        for k, g in enumerate(gs):
            place = places[k * clusters : (k + 1) * clusters]
            hot = jnp.concatenate(
                [jnp.where(slot_iota == place[c : c + 1, :], LOGIT_SCALE, 0.0) for c in range(clusters)],
                axis=0).astype(jnp.bfloat16)
            block = jnp.concatenate(
                [
                    jnp.concatenate(
                        [msg_ref[g * group + j, p * q : (p + 1) * q, :] for p in range(pieces)], axis=1)
                    for j in range(group)
                ],
                axis=0,
            )
            picks.append(jnp.dot(hot, block, preferred_element_type=jnp.float32).astype(jnp.bfloat16))
        for k, g in enumerate(gs):
            code[g] = places[k * clusters : (k + 1) * clusters]
            for c in range(clusters):
                qs[c, g] = picks[k][c * span : (c + 1) * span]
        return base

    slots = half * span
    class_iota = lax.broadcasted_iota(jnp.int32, (CLASSES, rows), 0)

    def score(c, base, buffer):
        picked = qs[c, pl.ds(base, half)].reshape(slots, depth)
        s_buf[buffer] = lax.dot_general(
            picked, bank_v[c], (((1,), (1,)), ((), ())), preferred_element_type=jnp.float32)

    def weigh(c, base, buffer):
        s = s_buf[buffer]
        top = jnp.max(s, axis=1, keepdims=True)
        e = jnp.exp(s - top)
        total = jnp.sum(e, axis=1, keepdims=True)
        hot = jnp.where(class_iota == labels_ref[pl.ds(c, 1), :], 1.0, 0.0).astype(jnp.bfloat16)
        tally = lax.dot_general(
            e.astype(jnp.bfloat16), hot, (((1,), (1,)), ((), ())), preferred_element_type=jnp.float32)
        where = pl.ds(base, half)
        top_b[c, where] = jnp.broadcast_to(top, (slots, LANES)).reshape(half, span, LANES)
        tot_b[c, where] = jnp.broadcast_to(total, (slots, LANES)).reshape(half, span, LANES)
        tal[c, where] = tally.reshape(half, span, CLASSES)

    def wait_bank(c):
        pltpu.make_async_copy(bank_ref.at[c], bank_v.at[c], bank_sem.at[c]).wait()

    def phase(base, near):
        if near:
            wait_bank(0)
        score(0, base, 0)

        def cluster(i, _):
            c = 2 * i
            if near:
                wait_bank(c + 1)
                wait_bank(c + 2)
                pl.when(c == clusters // 4)(serve_cross)
                pl.when(c == clusters // 2)(serve_corner)
            score(c + 1, base, 1)
            weigh(c, base, 0)
            score(c + 2, base, 0)
            weigh(c + 1, base, 1)
            return 0

        lax.fori_loop(0, clusters // 2 - 1, cluster, 0)
        if near:
            wait_bank(clusters - 1)
        score(clusters - 1, base, 1)
        weigh(clusters - 2, base, 0)
        weigh(clusters - 1, base, 1)

    def copies(g):
        target = device(g * group + my_place)
        return (
            pltpu.make_async_remote_copy(
                src_ref=send_t.at[g], dst_ref=recv_t.at[my_group], send_sem=st_sem.at[g],
                recv_sem=rt_sem.at[my_group], device_id=target, device_id_type=MESH),
            pltpu.make_async_remote_copy(
                src_ref=send_s.at[g], dst_ref=recv_s.at[my_group], send_sem=ss_sem.at[g],
                recv_sem=rs_sem.at[my_group], device_id=target, device_id_type=MESH),
        )

    wide = max(1, width // LANES)

    def merged_of(g):
        place = code[g]
        hots, tops = [], []
        for c in range(clusters):
            hot = slot_iota == place[c : c + 1, :]
            hots.append(hot)
            here = jnp.concatenate([top_b[c, g]] * wide, axis=1)
            tops.append(jnp.max(jnp.where(hot, here, LOW), axis=0, keepdims=True))
        highest = functools.reduce(jnp.maximum, tops)
        total = jnp.zeros((1, width), jnp.float32)
        scaled = []
        for c in range(clusters):
            w = jnp.exp(tops[c] - highest)
            here = jnp.concatenate([tot_b[c, g]] * wide, axis=1)
            total = total + w * jnp.sum(jnp.where(hots[c], here, 0.0), axis=0, keepdims=True)
            scaled.append(jnp.where(hots[c], w, 0.0))
        weight = jnp.concatenate(scaled, axis=0)
        tally = jnp.concatenate([tal[c, g] for c in range(clusters)], axis=0)
        w_hi = weight.astype(jnp.bfloat16)
        w_lo = (weight - w_hi.astype(jnp.float32)).astype(jnp.bfloat16)
        t_hi = tally.astype(jnp.bfloat16)
        t_lo = (tally - t_hi.astype(jnp.float32)).astype(jnp.bfloat16)

        def turn(a, b):
            return lax.dot_general(a, b, (((0,), (0,)), ((), ())), preferred_element_type=jnp.float32)

        merged = turn(t_hi, w_hi) + (turn(t_hi, w_lo) + turn(t_lo, w_hi))
        stats = jnp.concatenate([highest, total] + [jnp.zeros((1, width), jnp.float32)] * 6, axis=0)
        return merged.astype(jnp.bfloat16), stats

    def merge(i, base):
        gs = [base + lax.rem(my_group + 1 + i * batch + k, half) for k in range(batch)]
        done = [merged_of(g) for g in gs]
        for g, (merged, stats) in zip(gs, done):
            send_t[g] = merged
            send_s[g] = stats
        for g in gs:

            @pl.when(g != my_group)
            def _(g=g):
                for copy in copies(g):
                    copy.start()

        return base

    near_base = my_group // half * half
    far_base = half - near_base
    lax.fori_loop(0, half // batch, pick, near_base)
    phase(near_base, True)
    lax.fori_loop(0, half // batch, merge, near_base)
    for t in range(1, line):
        step_sibling(t, False)
    lax.fori_loop(0, half // batch, pick, far_base)
    phase(far_base, False)
    lax.fori_loop(0, half // batch, merge, far_base)

    def gathered(state, place):
        highest, total, merged = state
        stats, tally = place
        best = jnp.maximum(highest, stats[0:1, :])
        keep, w = jnp.exp(highest - best), jnp.exp(stats[0:1, :] - best)
        return (best, total * keep + w * stats[1:2, :], merged * keep + w * tally.astype(jnp.float32))

    def arrived(base):
        def one(j, state):
            g = base + lax.rem(my_group + 2 * half - j, half)
            for copy in (
                pltpu.make_async_remote_copy(
                    src_ref=send_t.at[g], dst_ref=recv_t.at[g], send_sem=st_sem.at[g], recv_sem=rt_sem.at[g],
                    device_id=device(g * group + my_place), device_id_type=MESH),
                pltpu.make_async_remote_copy(
                    src_ref=send_s.at[g], dst_ref=recv_s.at[g], send_sem=ss_sem.at[g], recv_sem=rs_sem.at[g],
                    device_id=device(g * group + my_place), device_id_type=MESH),
            ):
                copy.wait_recv()
            return gathered(state, (recv_s[g], recv_t[g]))

        return one

    own = send_s[my_group]
    state = (own[0:1, :], own[1:2, :], send_t[my_group].astype(jnp.float32))
    state = lax.fori_loop(1, half, arrived(near_base), state)
    state = lax.fori_loop(1, half + 1, arrived(far_base), state)
    highest, total, merged = state
    pair_out[0:CLASSES, :] = merged
    pair_out[CLASSES : CLASSES + 8, :] = jnp.concatenate(
        [highest, total] + [jnp.zeros((1, width), jnp.float32)] * 6, axis=0)

    def pair(j):
        return pltpu.make_async_remote_copy(
            src_ref=pair_out, dst_ref=pair_in.at[j], send_sem=ps_sem.at[j], recv_sem=pr_sem.at[j],
            device_id=device(my_group * group + lax.rem(my_place + j, group)), device_id_type=MESH)

    for j in range(1, group):
        pair(j).start()
    for j in range(1, group):
        pair(j).wait_recv()
    tops = [highest] + [pair_in[j, CLASSES : CLASSES + 1, :] for j in range(1, group)]
    best = functools.reduce(jnp.maximum, tops)
    w = jnp.exp(highest - best)
    total, merged = total * w, merged * w
    for j in range(1, group):
        w = jnp.exp(tops[j] - best)
        total = total + w * pair_in[j, CLASSES + 1 : CLASSES + 2, :]
        merged = merged + w * pair_in[j, 0:CLASSES, :]
    turned[...] = (merged / total).T
    out_ref[...] = turned[pl.ds(pl.multiple_of(my_place * q, q), q), :]

    ending.append(True)
    step_own()
    for t in range(line):
        if t >= 1:
            step_line(t)
        for near in (True, False):
            step_cross(t, near)
            step_corner(t, near)

    def sent(j, _):
        for copy in copies(lax.rem(my_group + j, groups)):
            copy.wait_send()
        return 0

    lax.fori_loop(1, groups, sent, 0)
    for j in range(1, group):
        pair(j).wait_send()


def local(queries, bank, labels, probes):
    q, depth = queries.shape
    probe_count = probes.shape[1]
    clusters, rows, _ = bank.shape
    n_dp, n_rep = lax.axis_size("dp"), lax.axis_size("rep")
    n = n_dp * n_rep
    cap = 2 * q * probe_count // (clusters * n_dp)
    group = max(LANES // q, 16 // cap)
    groups, width, span = n // group, group * q, group * cap
    pieces = depth // LANES

    cfg = (n_rep, n, q, cap, clusters, rows, depth, probe_count, group)
    vmem = pl.BlockSpec(memory_space=pltpu.VMEM)
    f32, bf16 = jnp.float32, jnp.bfloat16
    return pl.pallas_call(
        functools.partial(kernel, cfg),
        out_shape=jax.ShapeDtypeStruct((q, CLASSES), f32),
        in_specs=[vmem, vmem, vmem, pl.BlockSpec(memory_space=pl.ANY)],
        out_specs=vmem,
        scratch_shapes=[
            pltpu.VMEM((n, pieces * q + 16, LANES), bf16),
            pltpu.VMEM((clusters, rows, depth), bf16),
            pltpu.VMEM((groups, clusters, width), jnp.int32),
            pltpu.VMEM((clusters, groups, span, depth), bf16),
            pltpu.VMEM((2, groups // 2 * span, rows), f32),
            pltpu.VMEM((clusters, groups, span, LANES), f32),
            pltpu.VMEM((clusters, groups, span, LANES), f32),
            pltpu.VMEM((clusters, groups, span, CLASSES), f32),
            pltpu.VMEM((groups, CLASSES, width), bf16),
            pltpu.VMEM((groups, 8, width), f32),
            pltpu.VMEM((groups, CLASSES, width), bf16),
            pltpu.VMEM((groups, 8, width), f32),
            pltpu.VMEM((CLASSES + 8, width), f32),
            pltpu.VMEM((group, CLASSES + 8, width), f32),
            pltpu.VMEM((width, CLASSES), f32),
            pltpu.SemaphoreType.DMA((clusters,)),
            pltpu.SemaphoreType.DMA((n, 5)),
            pltpu.SemaphoreType.DMA((n, 2)),
            pltpu.SemaphoreType.DMA((groups,)),
            pltpu.SemaphoreType.DMA((groups,)),
            pltpu.SemaphoreType.DMA((groups,)),
            pltpu.SemaphoreType.DMA((groups,)),
            pltpu.SemaphoreType.DMA((group,)),
            pltpu.SemaphoreType.DMA((group,)),
        ],
        compiler_params=pltpu.CompilerParams(
            collective_id=0, has_side_effects=True, vmem_limit_bytes=56 * 1024 * 1024),
    )(queries, probes.T, labels, bank) * CLASSES


def solution(mesh):
    return jax.shard_map(
        local,
        mesh=mesh,
        in_specs=(
            P(("dp", "rep"), None),
            P("dp", "rep", None),
            P("dp", "rep"),
            P(("dp", "rep"), None),
        ),
        out_specs=P(("dp", "rep"), None),
        check_vma=False,
    )
```

```python
import functools

import jax
import jax.numpy as jnp
from jax import lax
from jax.experimental import pallas as pl
from jax.experimental.pallas import tpu as pltpu
from jax.sharding import PartitionSpec as P

CLASSES = 128
LANES = 128
LOGIT_SCALE = 2.0
LOW = -3.0e38
MESH = pl.DeviceIdType.MESH


def kernel(cfg, query_ref, probe_ref, labels_ref, bank_ref, out_ref,
           msg_ref, bank_v, code, qs, s_buf, top_b, tot_b, tal, send_t, send_s,
           recv_t, recv_s, pair_out, pair_in, turned,
           bank_sem, go_sem, come_sem, st_sem, ss_sem, rt_sem, rs_sem, ps_sem, pr_sem):
    n_rep, n, q, cap, clusters, rows, depth, probe_count, group = cfg
    groups, width, span = n // group, group * q, group * cap
    pieces = depth // LANES
    me_dp, me_rep = lax.axis_index("dp"), lax.axis_index("rep")
    me = me_dp * n_rep + me_rep
    my_group, my_place = me // group, lax.rem(me, group)

    def device(flat):
        return (flat // n_rep, lax.rem(flat, n_rep))

    for c in range(clusters):
        pltpu.make_async_copy(bank_ref.at[c], bank_v.at[c], bank_sem.at[c]).start()

    barrier = pltpu.get_barrier_semaphore()

    def greet(flat):
        pl.semaphore_signal(barrier, inc=1, device_id=device(flat), device_id_type=MESH)

    for j in range(1, groups):
        greet(lax.rem(my_group + j, groups) * group + my_place)
    for j in range(1, group):
        greet(my_group * group + lax.rem(my_place + j, group))
    pl.semaphore_wait(barrier, groups + group - 2)

    line, z, y = lax.axis_size("dp") // 2, me_dp // 2, lax.rem(me_dp, 2)
    x, core = me_rep // 2, lax.rem(me_rep, 2)
    height = pieces * q + 16
    cut = height // 32 * 16
    whole, upper, lower = (0, height), (0, cut), (cut, height - cut)

    def at(z_, y_, x_, core_):
        return (z_ * 2 + y_) * n_rep + x_ * 2 + core_

    def move(block, part, kind, target):
        return pltpu.make_async_remote_copy(
            src_ref=msg_ref.at[block, pl.ds(*part)], dst_ref=msg_ref.at[block, pl.ds(*part)],
            send_sem=go_sem.at[block, kind], recv_sem=come_sem.at[block, 1 if part == lower else 0],
            device_id=device(target), device_id_type=MESH)

    sibling, over_x, over_y = at(z, y, x, 1 - core), at(z, y, 1 - x, core), at(z, 1 - y, x, core)
    ending = []

    def start(condition, block, part, kind, target):
        def run():
            copy = move(block, part, kind, target)
            if ending:
                copy.wait_send()
            else:
                copy.start()

        pl.when(condition)(run)

    def wait_for(condition, block, part, source):
        def run():
            move(block, part, 0, source).wait_recv()

        if not ending:
            pl.when(condition)(run)

    def fan_out(b, there):
        block = at(b, y, x, core)
        start(there, block, whole, 2, over_x)
        start(there, block, whole, 3, over_y)
        start(there, block, whole, 4, sibling)

    def step_line(t):
        for b, there, source, onward, kind in (
            (z - t, z - t >= 0, z - 1, z + 1, 0),
            (z + t, z + t < line, z + 1, z - 1, 1),
        ):
            block = at(b, y, x, core)
            wait_for(there, block, whole, at(source, y, x, core))
            start(there & (onward >= 0) & (onward < line), block, whole, kind, at(onward, y, x, core))
            fan_out(b, there)

    def both(t, near):
        if t == 0:
            return ((z, z >= 0),) if near else ()
        spots = ((z - t, z - t >= 0), (z + t, z + t < line))
        mine = z // (line // 2)
        if near:
            return tuple((b, there & (b // (line // 2) == mine)) for b, there in spots)
        return tuple((b, there & (b // (line // 2) != mine)) for b, there in spots)

    def step_cross(t, near):
        for b, there in both(t, near):
            block = at(b, y, 1 - x, core)
            wait_for(there, block, whole, over_x)
            start(there, block, upper, 3, over_y)
            start(there, block, whole, 4, sibling)
            block = at(b, 1 - y, x, core)
            wait_for(there, block, whole, over_y)
            start(there, block, lower, 2, over_x)
            start(there, block, whole, 4, sibling)

    def step_corner(t, near):
        for b, there in both(t, near):
            block = at(b, 1 - y, 1 - x, core)
            wait_for(there, block, upper, over_y)
            start(there, block, upper, 3, sibling)
            wait_for(there, block, lower, over_x)
            start(there, block, lower, 4, sibling)

    def step_sibling(t, near):
        for b, there in both(t, near):
            wait_for(there, at(b, y, x, 1 - core), whole, sibling)
            wait_for(there, at(b, y, 1 - x, 1 - core), whole, sibling)
            wait_for(there, at(b, 1 - y, x, 1 - core), whole, sibling)
            wait_for(there, at(b, 1 - y, 1 - x, 1 - core), upper, sibling)
            wait_for(there, at(b, 1 - y, 1 - x, 1 - core), lower, sibling)

    for p in range(pieces):
        msg_ref[me, p * q : (p + 1) * q, :] = query_ref[:, p * LANES : (p + 1) * LANES]
    shift = my_place * q if width == LANES else 0
    spread = lax.broadcasted_iota(jnp.int32, (q, LANES), 1) == (
        lax.broadcasted_iota(jnp.int32, (q, LANES), 0) + shift)
    raised = jnp.concatenate(
        [(probe_ref[...] + 1).astype(jnp.float32), jnp.zeros((16 - probe_count, q), jnp.float32)],
        axis=0).astype(jnp.bfloat16)
    named_here = jnp.dot(
        raised, jnp.where(spread, 1.0, 0.0).astype(jnp.bfloat16), preferred_element_type=jnp.float32)
    msg_ref[me, pieces * q : height, :] = (named_here - 1.0).astype(jnp.bfloat16)

    def step_own():
        start(z + 1 < line, me, whole, 0, at(z + 1, y, x, core))
        start(z >= 1, me, whole, 1, at(z - 1, y, x, core))
        fan_out(z, z >= 0)

    step_own()
    close = line // 2
    for t in range(line):
        if t >= 1:
            step_line(t)
        if t < close:
            step_cross(t, True)
        if 1 <= t <= close:
            step_corner(t - 1, True)
    for t in range(close):
        step_sibling(t, True)

    def serve_cross():
        for t in range(1, line):
            step_cross(t, False)

    def serve_corner():
        for t in range(1, line):
            step_corner(t, False)

    lane = lax.broadcasted_iota(jnp.int32, (width, width), 1)
    row = lax.broadcasted_iota(jnp.int32, (width, width), 0)
    before = jnp.where((row < lane) & (row // q == lane // q), 1.0, 0.0).astype(jnp.bfloat16)
    offset = (lax.broadcasted_iota(jnp.int32, (1, width), 1) // q) * cap
    slot_iota = lax.broadcasted_iota(jnp.int32, (span, width), 0)
    first = me_dp * clusters
    probe_rows = 16
    half = groups // 2
    batch = 4 if half % 4 == 0 else 1

    def members_of(g):
        blocks = [msg_ref[g * group + j, pieces * q : pieces * q + probe_rows, :].astype(jnp.float32)
                  for j in range(group)]
        if width == LANES:
            named = functools.reduce(jnp.maximum, blocks)
        else:
            named = jnp.concatenate([block[:, :q] for block in blocks], axis=1)
        return [
            jnp.max(jnp.where(named == (first + c).astype(jnp.float32), 1.0, 0.0), axis=0, keepdims=True)
            for c in range(clusters)
        ]

    def pick(i, base):
        gs = [base + i * batch + k for k in range(batch)]
        member = jnp.concatenate([m for g in gs for m in members_of(g)], axis=0)
        rank = jnp.dot(member.astype(jnp.bfloat16), before, preferred_element_type=jnp.float32)
        places = jnp.where(member > 0.5, rank.astype(jnp.int32) + offset, -1)
        picks = []
        for k, g in enumerate(gs):
            place = places[k * clusters : (k + 1) * clusters]
            hot = jnp.concatenate(
                [jnp.where(slot_iota == place[c : c + 1, :], LOGIT_SCALE, 0.0) for c in range(clusters)],
                axis=0).astype(jnp.bfloat16)
            block = jnp.concatenate(
                [
                    jnp.concatenate(
                        [msg_ref[g * group + j, p * q : (p + 1) * q, :] for p in range(pieces)], axis=1)
                    for j in range(group)
                ],
                axis=0,
            )
            picks.append(jnp.dot(hot, block, preferred_element_type=jnp.float32).astype(jnp.bfloat16))
        for k, g in enumerate(gs):
            code[g] = places[k * clusters : (k + 1) * clusters]
            for c in range(clusters):
                qs[c, g] = picks[k][c * span : (c + 1) * span]
        return base

    slots = half * span
    class_iota = lax.broadcasted_iota(jnp.int32, (CLASSES, rows), 0)

    def score(c, base, buffer):
        picked = qs[c, pl.ds(base, half)].reshape(slots, depth)
        s_buf[buffer] = lax.dot_general(
            bank_v[c], picked, (((1,), (1,)), ((), ())), preferred_element_type=jnp.float32)

    def weigh(c, base, buffer):
        s = s_buf[buffer]
        top = jnp.max(s, axis=0, keepdims=True)
        e = jnp.exp(s - top)
        total = jnp.sum(e, axis=0, keepdims=True)
        hot = jnp.where(class_iota == labels_ref[pl.ds(c, 1), :], 1.0, 0.0).astype(jnp.bfloat16)
        tally = jnp.dot(hot, e.astype(jnp.bfloat16), preferred_element_type=jnp.float32)
        where = pl.ds(base, half)
        top_b[c, where] = jnp.broadcast_to(top, (LANES, slots)).T.reshape(half, span, LANES)
        tot_b[c, where] = jnp.broadcast_to(total, (LANES, slots)).T.reshape(half, span, LANES)
        tal[c, where] = tally.T.reshape(half, span, CLASSES)

    def wait_bank(c):
        pltpu.make_async_copy(bank_ref.at[c], bank_v.at[c], bank_sem.at[c]).wait()

    def phase(base, near):
        if near:
            wait_bank(0)
        score(0, base, 0)

        def cluster(i, _):
            c = 2 * i
            if near:
                wait_bank(c + 1)
                wait_bank(c + 2)
                pl.when(c == clusters // 4)(serve_cross)
                pl.when(c == clusters // 2)(serve_corner)
            score(c + 1, base, 1)
            weigh(c, base, 0)
            score(c + 2, base, 0)
            weigh(c + 1, base, 1)
            return 0

        lax.fori_loop(0, clusters // 2 - 1, cluster, 0)
        if near:
            wait_bank(clusters - 1)
        score(clusters - 1, base, 1)
        weigh(clusters - 2, base, 0)
        weigh(clusters - 1, base, 1)

    def copies(g):
        target = device(g * group + my_place)
        return (
            pltpu.make_async_remote_copy(
                src_ref=send_t.at[g], dst_ref=recv_t.at[my_group], send_sem=st_sem.at[g],
                recv_sem=rt_sem.at[my_group], device_id=target, device_id_type=MESH),
            pltpu.make_async_remote_copy(
                src_ref=send_s.at[g], dst_ref=recv_s.at[my_group], send_sem=ss_sem.at[g],
                recv_sem=rs_sem.at[my_group], device_id=target, device_id_type=MESH),
        )

    wide = max(1, width // LANES)

    def merged_of(g):
        place = code[g]
        hots, tops = [], []
        for c in range(clusters):
            hot = slot_iota == place[c : c + 1, :]
            hots.append(hot)
            here = jnp.concatenate([top_b[c, g]] * wide, axis=1)
            tops.append(jnp.max(jnp.where(hot, here, LOW), axis=0, keepdims=True))
        highest = functools.reduce(jnp.maximum, tops)
        total = jnp.zeros((1, width), jnp.float32)
        scaled = []
        for c in range(clusters):
            w = jnp.exp(tops[c] - highest)
            here = jnp.concatenate([tot_b[c, g]] * wide, axis=1)
            total = total + w * jnp.sum(jnp.where(hots[c], here, 0.0), axis=0, keepdims=True)
            scaled.append(jnp.where(hots[c], w, 0.0))
        weight = jnp.concatenate(scaled, axis=0)
        tally = jnp.concatenate([tal[c, g] for c in range(clusters)], axis=0)
        w_hi = weight.astype(jnp.bfloat16)
        w_lo = (weight - w_hi.astype(jnp.float32)).astype(jnp.bfloat16)
        t_hi = tally.astype(jnp.bfloat16)
        t_lo = (tally - t_hi.astype(jnp.float32)).astype(jnp.bfloat16)

        def turn(a, b):
            return lax.dot_general(a, b, (((0,), (0,)), ((), ())), preferred_element_type=jnp.float32)

        merged = turn(t_hi, w_hi) + (turn(t_hi, w_lo) + turn(t_lo, w_hi))
        stats = jnp.concatenate([highest, total] + [jnp.zeros((1, width), jnp.float32)] * 6, axis=0)
        return merged.astype(jnp.bfloat16), stats

    def merge(i, base):
        gs = [base + lax.rem(my_group + 1 + i * batch + k, half) for k in range(batch)]
        done = [merged_of(g) for g in gs]
        for g, (merged, stats) in zip(gs, done):
            send_t[g] = merged
            send_s[g] = stats
        for g in gs:

            @pl.when(g != my_group)
            def _(g=g):
                for copy in copies(g):
                    copy.start()

        return base

    near_base = my_group // half * half
    far_base = half - near_base
    lax.fori_loop(0, half // batch, pick, near_base)
    phase(near_base, True)
    lax.fori_loop(0, half // batch, merge, near_base)
    for t in range(1, line):
        step_sibling(t, False)
    lax.fori_loop(0, half // batch, pick, far_base)
    phase(far_base, False)
    lax.fori_loop(0, half // batch, merge, far_base)

    def gathered(state, place):
        highest, total, merged = state
        stats, tally = place
        best = jnp.maximum(highest, stats[0:1, :])
        keep, w = jnp.exp(highest - best), jnp.exp(stats[0:1, :] - best)
        return (best, total * keep + w * stats[1:2, :], merged * keep + w * tally.astype(jnp.float32))

    def arrived(base):
        def one(j, state):
            g = base + lax.rem(my_group + 2 * half - j, half)
            for copy in (
                pltpu.make_async_remote_copy(
                    src_ref=send_t.at[g], dst_ref=recv_t.at[g], send_sem=st_sem.at[g], recv_sem=rt_sem.at[g],
                    device_id=device(g * group + my_place), device_id_type=MESH),
                pltpu.make_async_remote_copy(
                    src_ref=send_s.at[g], dst_ref=recv_s.at[g], send_sem=ss_sem.at[g], recv_sem=rs_sem.at[g],
                    device_id=device(g * group + my_place), device_id_type=MESH),
            ):
                copy.wait_recv()
            return gathered(state, (recv_s[g], recv_t[g]))

        return one

    own = send_s[my_group]
    state = (own[0:1, :], own[1:2, :], send_t[my_group].astype(jnp.float32))
    state = lax.fori_loop(1, half, arrived(near_base), state)
    state = lax.fori_loop(1, half + 1, arrived(far_base), state)
    highest, total, merged = state
    pair_out[0:CLASSES, :] = merged
    pair_out[CLASSES : CLASSES + 8, :] = jnp.concatenate(
        [highest, total] + [jnp.zeros((1, width), jnp.float32)] * 6, axis=0)

    def pair(j):
        return pltpu.make_async_remote_copy(
            src_ref=pair_out, dst_ref=pair_in.at[j], send_sem=ps_sem.at[j], recv_sem=pr_sem.at[j],
            device_id=device(my_group * group + lax.rem(my_place + j, group)), device_id_type=MESH)

    for j in range(1, group):
        pair(j).start()
    for j in range(1, group):
        pair(j).wait_recv()
    tops = [highest] + [pair_in[j, CLASSES : CLASSES + 1, :] for j in range(1, group)]
    best = functools.reduce(jnp.maximum, tops)
    w = jnp.exp(highest - best)
    total, merged = total * w, merged * w
    for j in range(1, group):
        w = jnp.exp(tops[j] - best)
        total = total + w * pair_in[j, CLASSES + 1 : CLASSES + 2, :]
        merged = merged + w * pair_in[j, 0:CLASSES, :]
    turned[...] = (merged / total).T
    out_ref[...] = turned[pl.ds(pl.multiple_of(my_place * q, q), q), :]

    ending.append(True)
    step_own()
    for t in range(line):
        if t >= 1:
            step_line(t)
        for near in (True, False):
            step_cross(t, near)
            step_corner(t, near)

    def sent(j, _):
        for copy in copies(lax.rem(my_group + j, groups)):
            copy.wait_send()
        return 0

    lax.fori_loop(1, groups, sent, 0)
    for j in range(1, group):
        pair(j).wait_send()


def local(queries, bank, labels, probes):
    q, depth = queries.shape
    probe_count = probes.shape[1]
    clusters, rows, _ = bank.shape
    n_dp, n_rep = lax.axis_size("dp"), lax.axis_size("rep")
    n = n_dp * n_rep
    cap = 2 * q * probe_count // (clusters * n_dp)
    group = max(LANES // q, 16 // cap)
    groups, width, span = n // group, group * q, group * cap
    pieces = depth // LANES

    cfg = (n_rep, n, q, cap, clusters, rows, depth, probe_count, group)
    vmem = pl.BlockSpec(memory_space=pltpu.VMEM)
    f32, bf16 = jnp.float32, jnp.bfloat16
    return pl.pallas_call(
        functools.partial(kernel, cfg),
        out_shape=jax.ShapeDtypeStruct((q, CLASSES), f32),
        in_specs=[vmem, vmem, vmem, pl.BlockSpec(memory_space=pl.ANY)],
        out_specs=vmem,
        scratch_shapes=[
            pltpu.VMEM((n, pieces * q + 16, LANES), bf16),
            pltpu.VMEM((clusters, rows, depth), bf16),
            pltpu.VMEM((groups, clusters, width), jnp.int32),
            pltpu.VMEM((clusters, groups, span, depth), bf16),
            pltpu.VMEM((2, rows, groups // 2 * span), f32),
            pltpu.VMEM((clusters, groups, span, LANES), f32),
            pltpu.VMEM((clusters, groups, span, LANES), f32),
            pltpu.VMEM((clusters, groups, span, CLASSES), f32),
            pltpu.VMEM((groups, CLASSES, width), bf16),
            pltpu.VMEM((groups, 8, width), f32),
            pltpu.VMEM((groups, CLASSES, width), bf16),
            pltpu.VMEM((groups, 8, width), f32),
            pltpu.VMEM((CLASSES + 8, width), f32),
            pltpu.VMEM((group, CLASSES + 8, width), f32),
            pltpu.VMEM((width, CLASSES), f32),
            pltpu.SemaphoreType.DMA((clusters,)),
            pltpu.SemaphoreType.DMA((n, 5)),
            pltpu.SemaphoreType.DMA((n, 2)),
            pltpu.SemaphoreType.DMA((groups,)),
            pltpu.SemaphoreType.DMA((groups,)),
            pltpu.SemaphoreType.DMA((groups,)),
            pltpu.SemaphoreType.DMA((groups,)),
            pltpu.SemaphoreType.DMA((group,)),
            pltpu.SemaphoreType.DMA((group,)),
        ],
        compiler_params=pltpu.CompilerParams(
            collective_id=0, has_side_effects=True, vmem_limit_bytes=56 * 1024 * 1024),
    )(queries, probes.T, labels, bank) * CLASSES


def solution(mesh):
    return jax.shard_map(
        local,
        mesh=mesh,
        in_specs=(
            P(("dp", "rep"), None),
            P("dp", "rep", None),
            P("dp", "rep"),
            P(("dp", "rep"), None),
        ),
        out_specs=P(("dp", "rep"), None),
        check_vma=False,
    )
```

```python
import functools

import jax
import jax.numpy as jnp
from jax import lax
from jax.experimental import pallas as pl
from jax.experimental.pallas import tpu as pltpu
from jax.sharding import PartitionSpec as P

CLASSES = 128
LANES = 128
LOGIT_SCALE = 2.0
LOW = -3.0e38
MESH = pl.DeviceIdType.MESH


def kernel(cfg, query_ref, probe_ref, labels_ref, bank_ref, out_ref,
           msg_ref, bank_v, code, qs, s_buf, top_b, tot_b, tal, send_t, send_s, give, keep, take,
           recv_t, recv_s, pair_out, pair_in, turned,
           bank_sem, go_sem, come_sem, st_sem, ss_sem, rt_sem, rs_sem, gs_sem, gr_sem, ps_sem, pr_sem):
    n_rep, n, q, cap, clusters, rows, depth, probe_count, group = cfg
    groups, width, span = n // group, group * q, group * cap
    pieces = depth // LANES
    me_dp, me_rep = lax.axis_index("dp"), lax.axis_index("rep")
    me = me_dp * n_rep + me_rep
    my_group, my_place = me // group, lax.rem(me, group)

    def device(flat):
        return (flat // n_rep, lax.rem(flat, n_rep))

    for c in range(clusters):
        pltpu.make_async_copy(bank_ref.at[c], bank_v.at[c], bank_sem.at[c]).start()

    barrier = pltpu.get_barrier_semaphore()

    def greet(flat):
        pl.semaphore_signal(barrier, inc=1, device_id=device(flat), device_id_type=MESH)

    for j in range(1, groups):
        greet(lax.rem(my_group + j, groups) * group + my_place)
    for j in range(1, group):
        greet(my_group * group + lax.rem(my_place + j, group))
    pl.semaphore_wait(barrier, groups + group - 2)

    line, z, y = lax.axis_size("dp") // 2, me_dp // 2, lax.rem(me_dp, 2)
    x, core = me_rep // 2, lax.rem(me_rep, 2)
    height = pieces * q + 16
    cut = height // 32 * 16
    whole, upper, lower = (0, height), (0, cut), (cut, height - cut)

    def at(z_, y_, x_, core_):
        return (z_ * 2 + y_) * n_rep + x_ * 2 + core_

    def move(block, part, kind, target):
        return pltpu.make_async_remote_copy(
            src_ref=msg_ref.at[block, pl.ds(*part)], dst_ref=msg_ref.at[block, pl.ds(*part)],
            send_sem=go_sem.at[block, kind], recv_sem=come_sem.at[block, 1 if part == lower else 0],
            device_id=device(target), device_id_type=MESH)

    sibling, over_x, over_y = at(z, y, x, 1 - core), at(z, y, 1 - x, core), at(z, 1 - y, x, core)
    ending = []

    def start(condition, block, part, kind, target):
        def run():
            copy = move(block, part, kind, target)
            if ending:
                copy.wait_send()
            else:
                copy.start()

        pl.when(condition)(run)

    def wait_for(condition, block, part, source):
        def run():
            move(block, part, 0, source).wait_recv()

        if not ending:
            pl.when(condition)(run)

    def fan_out(b, there):
        block = at(b, y, x, core)
        start(there, block, whole, 2, over_x)
        start(there, block, whole, 3, over_y)
        start(there, block, whole, 4, sibling)

    def step_line(t):
        for b, there, source, onward, kind in (
            (z - t, z - t >= 0, z - 1, z + 1, 0),
            (z + t, z + t < line, z + 1, z - 1, 1),
        ):
            block = at(b, y, x, core)
            wait_for(there, block, whole, at(source, y, x, core))
            start(there & (onward >= 0) & (onward < line), block, whole, kind, at(onward, y, x, core))
            fan_out(b, there)

    def both(t, near):
        if t == 0:
            return ((z, z >= 0),) if near else ()
        spots = ((z - t, z - t >= 0), (z + t, z + t < line))
        mine = z // (line // 2)
        if near:
            return tuple((b, there & (b // (line // 2) == mine)) for b, there in spots)
        return tuple((b, there & (b // (line // 2) != mine)) for b, there in spots)

    def step_cross(t, near):
        for b, there in both(t, near):
            block = at(b, y, 1 - x, core)
            wait_for(there, block, whole, over_x)
            start(there, block, upper, 3, over_y)
            start(there, block, whole, 4, sibling)
            block = at(b, 1 - y, x, core)
            wait_for(there, block, whole, over_y)
            start(there, block, lower, 2, over_x)
            start(there, block, whole, 4, sibling)

    def step_corner(t, near):
        for b, there in both(t, near):
            block = at(b, 1 - y, 1 - x, core)
            wait_for(there, block, upper, over_y)
            start(there, block, upper, 3, sibling)
            wait_for(there, block, lower, over_x)
            start(there, block, lower, 4, sibling)

    def step_sibling(t, near):
        for b, there in both(t, near):
            wait_for(there, at(b, y, x, 1 - core), whole, sibling)
            wait_for(there, at(b, y, 1 - x, 1 - core), whole, sibling)
            wait_for(there, at(b, 1 - y, x, 1 - core), whole, sibling)
            wait_for(there, at(b, 1 - y, 1 - x, 1 - core), upper, sibling)
            wait_for(there, at(b, 1 - y, 1 - x, 1 - core), lower, sibling)

    for p in range(pieces):
        msg_ref[me, p * q : (p + 1) * q, :] = query_ref[:, p * LANES : (p + 1) * LANES]
    shift = my_place * q if width == LANES else 0
    spread = lax.broadcasted_iota(jnp.int32, (q, LANES), 1) == (
        lax.broadcasted_iota(jnp.int32, (q, LANES), 0) + shift)
    raised = jnp.concatenate(
        [(probe_ref[...] + 1).astype(jnp.float32), jnp.zeros((16 - probe_count, q), jnp.float32)],
        axis=0).astype(jnp.bfloat16)
    named_here = jnp.dot(
        raised, jnp.where(spread, 1.0, 0.0).astype(jnp.bfloat16), preferred_element_type=jnp.float32)
    msg_ref[me, pieces * q : height, :] = (named_here - 1.0).astype(jnp.bfloat16)

    def step_own():
        start(z + 1 < line, me, whole, 0, at(z + 1, y, x, core))
        start(z >= 1, me, whole, 1, at(z - 1, y, x, core))
        fan_out(z, z >= 0)

    step_own()
    close = line // 2
    for t in range(line):
        if t >= 1:
            step_line(t)
        if t < close:
            step_cross(t, True)
        if 1 <= t <= close:
            step_corner(t - 1, True)
    for t in range(close):
        step_sibling(t, True)

    def serve_cross():
        for t in range(1, line):
            step_cross(t, False)

    def serve_corner():
        for t in range(1, line):
            step_corner(t, False)

    lane = lax.broadcasted_iota(jnp.int32, (width, width), 1)
    row = lax.broadcasted_iota(jnp.int32, (width, width), 0)
    before = jnp.where((row < lane) & (row // q == lane // q), 1.0, 0.0).astype(jnp.bfloat16)
    offset = (lax.broadcasted_iota(jnp.int32, (1, width), 1) // q) * cap
    slot_iota = lax.broadcasted_iota(jnp.int32, (span, width), 0)
    first = me_dp * clusters
    probe_rows = 16
    half = groups // 2
    batch = 4 if half % 4 == 0 else 1

    def members_of(g):
        blocks = [msg_ref[g * group + j, pieces * q : pieces * q + probe_rows, :].astype(jnp.float32)
                  for j in range(group)]
        if width == LANES:
            named = functools.reduce(jnp.maximum, blocks)
        else:
            named = jnp.concatenate([block[:, :q] for block in blocks], axis=1)
        return [
            jnp.max(jnp.where(named == (first + c).astype(jnp.float32), 1.0, 0.0), axis=0, keepdims=True)
            for c in range(clusters)
        ]

    def pick(i, base):
        gs = [base + i * batch + k for k in range(batch)]
        member = jnp.concatenate([m for g in gs for m in members_of(g)], axis=0)
        rank = jnp.dot(member.astype(jnp.bfloat16), before, preferred_element_type=jnp.float32)
        places = jnp.where(member > 0.5, rank.astype(jnp.int32) + offset, -1)
        picks = []
        for k, g in enumerate(gs):
            place = places[k * clusters : (k + 1) * clusters]
            hot = jnp.concatenate(
                [jnp.where(slot_iota == place[c : c + 1, :], LOGIT_SCALE, 0.0) for c in range(clusters)],
                axis=0).astype(jnp.bfloat16)
            block = jnp.concatenate(
                [
                    jnp.concatenate(
                        [msg_ref[g * group + j, p * q : (p + 1) * q, :] for p in range(pieces)], axis=1)
                    for j in range(group)
                ],
                axis=0,
            )
            picks.append(jnp.dot(hot, block, preferred_element_type=jnp.float32).astype(jnp.bfloat16))
        for k, g in enumerate(gs):
            code[g] = places[k * clusters : (k + 1) * clusters]
            for c in range(clusters):
                qs[c, g] = picks[k][c * span : (c + 1) * span]
        return base

    slots = half * span
    class_iota = lax.broadcasted_iota(jnp.int32, (CLASSES, rows), 0)

    def score(c, base, buffer):
        picked = qs[c, pl.ds(base, half)].reshape(slots, depth)
        s_buf[buffer] = lax.dot_general(
            picked, bank_v[c], (((1,), (1,)), ((), ())), preferred_element_type=jnp.float32)

    def weigh(c, base, buffer):
        s = s_buf[buffer]
        top = jnp.max(s, axis=1, keepdims=True)
        e = jnp.exp(s - top)
        total = jnp.sum(e, axis=1, keepdims=True)
        hot = jnp.where(class_iota == labels_ref[pl.ds(c, 1), :], 1.0, 0.0).astype(jnp.bfloat16)
        tally = lax.dot_general(
            e.astype(jnp.bfloat16), hot, (((1,), (1,)), ((), ())), preferred_element_type=jnp.float32)
        where = pl.ds(base, half)
        top_b[c, where] = jnp.broadcast_to(top, (slots, LANES)).reshape(half, span, LANES)
        tot_b[c, where] = jnp.broadcast_to(total, (slots, LANES)).reshape(half, span, LANES)
        tal[c, where] = tally.reshape(half, span, CLASSES)

    def wait_bank(c):
        pltpu.make_async_copy(bank_ref.at[c], bank_v.at[c], bank_sem.at[c]).wait()

    def phase(base, near):
        if near:
            wait_bank(0)
        score(0, base, 0)

        def cluster(i, _):
            c = 2 * i
            if near:
                wait_bank(c + 1)
                wait_bank(c + 2)
                pl.when(c == 0)(serve_cross)
                pl.when(c == clusters // 4)(serve_corner)
            score(c + 1, base, 1)
            weigh(c, base, 0)
            score(c + 2, base, 0)
            weigh(c + 1, base, 1)
            return 0

        lax.fori_loop(0, clusters // 2 - 1, cluster, 0)
        if near:
            wait_bank(clusters - 1)
        score(clusters - 1, base, 1)
        weigh(clusters - 2, base, 0)
        weigh(clusters - 1, base, 1)

    def copies(g):
        target = device(g * group + my_place)
        return (
            pltpu.make_async_remote_copy(
                src_ref=send_t.at[g], dst_ref=recv_t.at[my_group], send_sem=st_sem.at[g],
                recv_sem=rt_sem.at[my_group], device_id=target, device_id_type=MESH),
            pltpu.make_async_remote_copy(
                src_ref=send_s.at[g], dst_ref=recv_s.at[my_group], send_sem=ss_sem.at[g],
                recv_sem=rs_sem.at[my_group], device_id=target, device_id_type=MESH),
        )

    wide = max(1, width // LANES)

    def merged_of(g):
        place = code[g]
        hots, tops = [], []
        for c in range(clusters):
            hot = slot_iota == place[c : c + 1, :]
            hots.append(hot)
            here = jnp.concatenate([top_b[c, g]] * wide, axis=1)
            tops.append(jnp.max(jnp.where(hot, here, LOW), axis=0, keepdims=True))
        highest = functools.reduce(jnp.maximum, tops)
        total = jnp.zeros((1, width), jnp.float32)
        scaled = []
        for c in range(clusters):
            w = jnp.exp(tops[c] - highest)
            here = jnp.concatenate([tot_b[c, g]] * wide, axis=1)
            total = total + w * jnp.sum(jnp.where(hots[c], here, 0.0), axis=0, keepdims=True)
            scaled.append(jnp.where(hots[c], w, 0.0))
        weight = jnp.concatenate(scaled, axis=0)
        tally = jnp.concatenate([tal[c, g] for c in range(clusters)], axis=0)
        w_hi = weight.astype(jnp.bfloat16)
        w_lo = (weight - w_hi.astype(jnp.float32)).astype(jnp.bfloat16)
        t_hi = tally.astype(jnp.bfloat16)
        t_lo = (tally - t_hi.astype(jnp.float32)).astype(jnp.bfloat16)

        def turn(a, b):
            return lax.dot_general(a, b, (((0,), (0,)), ((), ())), preferred_element_type=jnp.float32)

        merged = turn(t_hi, w_hi) + (turn(t_hi, w_lo) + turn(t_lo, w_hi))
        stats = jnp.concatenate([highest, total] + [jnp.zeros((1, width), jnp.float32)] * 6, axis=0)
        return merged, stats

    def merge(i, base):
        gs = [base + lax.rem(my_group + 1 + i * batch + k, half) for k in range(batch)]
        done = [merged_of(g) for g in gs]
        for g, (merged, stats) in zip(gs, done):
            send_t[g] = merged.astype(jnp.bfloat16)
            send_s[g] = stats
        for g in gs:

            @pl.when(g != my_group)
            def _(g=g):
                for copy in copies(g):
                    copy.start()

        return base

    def hand_over(k):
        return pltpu.make_async_remote_copy(
            src_ref=give.at[k], dst_ref=take.at[k], send_sem=gs_sem.at[k], recv_sem=gr_sem.at[k],
            device_id=device(sibling), device_id_type=MESH)

    shared = half // 2
    chunk = 4 if shared % 4 == 0 else 1

    def merge_shared(i, base, buffer, parity):
        ks = [i * chunk + k for k in range(chunk)]
        done = [merged_of(base + 2 * k + parity) for k in ks]
        for k, (merged, stats) in zip(ks, done):
            buffer[k, 0:CLASSES, :] = merged
            buffer[k, CLASSES : CLASSES + 8, :] = stats

    def merge_give(i, base):
        merge_shared(i, base, give, 1 - core)
        for k in range(chunk):
            hand_over(i * chunk + k).start()
        return base

    def merge_keep(i, base):
        merge_shared(i, base, keep, core)
        return base

    def merge_both(i, base):
        k = lax.rem(my_group + i, shared)
        g = base + 2 * k + core
        hand_over(k).wait_recv()
        mine, theirs = keep[k], take[k]
        top_m, top_t = mine[CLASSES : CLASSES + 1], theirs[CLASSES : CLASSES + 1]
        best = jnp.maximum(top_m, top_t)
        w_m, w_t = jnp.exp(top_m - best), jnp.exp(top_t - best)
        send_t[g] = (mine[0:CLASSES] * w_m + theirs[0:CLASSES] * w_t).astype(jnp.bfloat16)
        total = mine[CLASSES + 1 : CLASSES + 2] * w_m + theirs[CLASSES + 1 : CLASSES + 2] * w_t
        send_s[g] = jnp.concatenate([best, total] + [jnp.zeros((1, width), jnp.float32)] * 6, axis=0)
        for copy in copies(g):
            copy.start()
        return base

    near_base = my_group // half * half
    far_base = half - near_base
    lax.fori_loop(0, half // batch, pick, near_base)
    phase(near_base, True)
    lax.fori_loop(0, half // batch, merge, near_base)
    for t in range(1, line):
        step_sibling(t, False)
    lax.fori_loop(0, half // batch, pick, far_base)
    phase(far_base, False)
    lax.fori_loop(0, shared // chunk, merge_give, far_base)
    lax.fori_loop(0, shared // chunk, merge_keep, far_base)
    lax.fori_loop(0, shared, merge_both, far_base)

    def gathered(state, place):
        highest, total, merged = state
        stats, tally = place
        best = jnp.maximum(highest, stats[0:1, :])
        keep, w = jnp.exp(highest - best), jnp.exp(stats[0:1, :] - best)
        return (best, total * keep + w * stats[1:2, :], merged * keep + w * tally.astype(jnp.float32))

    def arrived(base):
        def one(j, state):
            g = base + lax.rem(my_group + 2 * half - j, half)
            for copy in (
                pltpu.make_async_remote_copy(
                    src_ref=send_t.at[g], dst_ref=recv_t.at[g], send_sem=st_sem.at[g], recv_sem=rt_sem.at[g],
                    device_id=device(g * group + my_place), device_id_type=MESH),
                pltpu.make_async_remote_copy(
                    src_ref=send_s.at[g], dst_ref=recv_s.at[g], send_sem=ss_sem.at[g], recv_sem=rs_sem.at[g],
                    device_id=device(g * group + my_place), device_id_type=MESH),
            ):
                copy.wait_recv()
            return gathered(state, (recv_s[g], recv_t[g]))

        return one

    own = send_s[my_group]
    state = (own[0:1, :], own[1:2, :], send_t[my_group].astype(jnp.float32))
    state = lax.fori_loop(1, half, arrived(near_base), state)
    served = lax.rem(lax.rem(my_group, half), 2) == core
    state = lax.fori_loop(1, 1 + jnp.where(served, half, 0), arrived(far_base), state)
    highest, total, merged = state
    pair_out[0:CLASSES, :] = merged
    pair_out[CLASSES : CLASSES + 8, :] = jnp.concatenate(
        [highest, total] + [jnp.zeros((1, width), jnp.float32)] * 6, axis=0)

    def pair(j):
        return pltpu.make_async_remote_copy(
            src_ref=pair_out, dst_ref=pair_in.at[j], send_sem=ps_sem.at[j], recv_sem=pr_sem.at[j],
            device_id=device(my_group * group + lax.rem(my_place + j, group)), device_id_type=MESH)

    for j in range(1, group):
        pair(j).start()
    for j in range(1, group):
        pair(j).wait_recv()
    tops = [highest] + [pair_in[j, CLASSES : CLASSES + 1, :] for j in range(1, group)]
    best = functools.reduce(jnp.maximum, tops)
    w = jnp.exp(highest - best)
    total, merged = total * w, merged * w
    for j in range(1, group):
        w = jnp.exp(tops[j] - best)
        total = total + w * pair_in[j, CLASSES + 1 : CLASSES + 2, :]
        merged = merged + w * pair_in[j, 0:CLASSES, :]
    turned[...] = (merged / total).T
    out_ref[...] = turned[pl.ds(pl.multiple_of(my_place * q, q), q), :]

    ending.append(True)
    step_own()
    for t in range(line):
        if t >= 1:
            step_line(t)
        for near in (True, False):
            step_cross(t, near)
            step_corner(t, near)

    def sent_near(j, base):
        for copy in copies(base + lax.rem(my_group + j, half)):
            copy.wait_send()
        return base

    def sent_far(k, base):
        hand_over(k).wait_send()
        for copy in copies(base + 2 * k + core):
            copy.wait_send()
        return base

    lax.fori_loop(1, half, sent_near, near_base)
    lax.fori_loop(0, shared, sent_far, far_base)
    for j in range(1, group):
        pair(j).wait_send()


def local(queries, bank, labels, probes):
    q, depth = queries.shape
    probe_count = probes.shape[1]
    clusters, rows, _ = bank.shape
    n_dp, n_rep = lax.axis_size("dp"), lax.axis_size("rep")
    n = n_dp * n_rep
    cap = 2 * q * probe_count // (clusters * n_dp)
    group = max(LANES // q, 16 // cap)
    groups, width, span = n // group, group * q, group * cap
    pieces = depth // LANES

    cfg = (n_rep, n, q, cap, clusters, rows, depth, probe_count, group)
    vmem = pl.BlockSpec(memory_space=pltpu.VMEM)
    f32, bf16 = jnp.float32, jnp.bfloat16
    return pl.pallas_call(
        functools.partial(kernel, cfg),
        out_shape=jax.ShapeDtypeStruct((q, CLASSES), f32),
        in_specs=[vmem, vmem, vmem, pl.BlockSpec(memory_space=pl.ANY)],
        out_specs=vmem,
        scratch_shapes=[
            pltpu.VMEM((n, pieces * q + 16, LANES), bf16),
            pltpu.VMEM((clusters, rows, depth), bf16),
            pltpu.VMEM((groups, clusters, width), jnp.int32),
            pltpu.VMEM((clusters, groups, span, depth), bf16),
            pltpu.VMEM((2, groups // 2 * span, rows), f32),
            pltpu.VMEM((clusters, groups, span, LANES), f32),
            pltpu.VMEM((clusters, groups, span, LANES), f32),
            pltpu.VMEM((clusters, groups, span, CLASSES), f32),
            pltpu.VMEM((groups, CLASSES, width), bf16),
            pltpu.VMEM((groups, 8, width), f32),
            pltpu.VMEM((groups // 4, CLASSES + 8, width), f32),
            pltpu.VMEM((groups // 4, CLASSES + 8, width), f32),
            pltpu.VMEM((groups // 4, CLASSES + 8, width), f32),
            pltpu.VMEM((groups, CLASSES, width), bf16),
            pltpu.VMEM((groups, 8, width), f32),
            pltpu.VMEM((CLASSES + 8, width), f32),
            pltpu.VMEM((group, CLASSES + 8, width), f32),
            pltpu.VMEM((width, CLASSES), f32),
            pltpu.SemaphoreType.DMA((clusters,)),
            pltpu.SemaphoreType.DMA((n, 5)),
            pltpu.SemaphoreType.DMA((n, 2)),
            pltpu.SemaphoreType.DMA((groups,)),
            pltpu.SemaphoreType.DMA((groups,)),
            pltpu.SemaphoreType.DMA((groups,)),
            pltpu.SemaphoreType.DMA((groups,)),
            pltpu.SemaphoreType.DMA((groups // 4,)),
            pltpu.SemaphoreType.DMA((groups // 4,)),
            pltpu.SemaphoreType.DMA((group,)),
            pltpu.SemaphoreType.DMA((group,)),
        ],
        compiler_params=pltpu.CompilerParams(
            collective_id=0, has_side_effects=True, vmem_limit_bytes=56 * 1024 * 1024),
    )(queries, probes.T, labels, bank) * CLASSES


def solution(mesh):
    return jax.shard_map(
        local,
        mesh=mesh,
        in_specs=(
            P(("dp", "rep"), None),
            P("dp", "rep", None),
            P("dp", "rep"),
            P(("dp", "rep"), None),
        ),
        out_specs=P(("dp", "rep"), None),
        check_vma=False,
    )
```
